128 devices in a mesh: ctx: 8 (over z_hi, x), tp: 8 (over y, core), section: 2 (over z_lo).
Axes of the slice: x: 4, y: 4, z: 4 (z_hi: 2, z_lo: 2; z = z_hi * 2 + z_lo), core: 2. Of those that a mesh axis runs over, the one named last changes fastest.
Arguments:
- prompt_mixer: bfloat16 [8192, 16384], P(('ctx', 'section'), 'tp'), may hold values from -5 to 5
- prompt_gates: bfloat16 [8192, 16384], P(('ctx', 'section'), 'tp'), may hold values from -5 to 5
- prompt_write: bfloat16 [8192, 2048], P(('ctx', 'section'), 'tp'), may hold values from -5 to 5
- prompt_read: bfloat16 [8192, 2048], P(('ctx', 'section'), 'tp'), may hold values from -1 to 1
- prompt_steps: float32 [8192, 256], P(('ctx', 'section'), 'tp'), may hold values from 0 to 1, as said below
- decay_logs: float32 [256], P('tp'), may hold values from -12 to 0
- skip_weights: float32 [256], P('tp'), may hold values from 0.5 to 1.5
- norm_gains: float32 [16384], P('tp'), may hold values from 0.1 to 1.9
- prompt_keys: bfloat16 [8192, 1024], P(('ctx', 'section'), 'tp'), may hold values from -4 to 4
- prompt_values: bfloat16 [8192, 1024], P(('ctx', 'section'), 'tp'), may hold values from -5 to 5
- page_counts: int32 [128], replicated, may hold values from 1 to 16, as said below
- decode_mixer: bfloat16 [128, 4, 16384], P(('ctx', 'section'), None, 'tp'), may hold values from -5 to 5
- decode_gates: bfloat16 [128, 4, 16384], P(('ctx', 'section'), None, 'tp'), may hold values from -5 to 5
- decode_write: bfloat16 [128, 4, 2048], P(('ctx', 'section'), None, 'tp'), may hold values from -5 to 5
- decode_read: bfloat16 [128, 4, 2048], P(('ctx', 'section'), None, 'tp'), may hold values from -1 to 1
- decode_steps: float32 [128, 4, 256], P(('ctx', 'section'), None, 'tp'), may hold values from 0 to 1, as said below
- decode_queries: bfloat16 [128, 4, 8192], P(('ctx', 'section'), None, 'tp'), may hold values from -150 to 150
- decode_keys: bfloat16 [128, 4, 1024], P(('ctx', 'section'), None, 'tp'), may hold values from -5 to 5
- decode_values: bfloat16 [128, 4, 1024], P(('ctx', 'section'), None, 'tp'), may hold values from -5 to 5
- mixer_output: bfloat16 [16384, 8192], P('tp', ('ctx', 'section')), may hold values from -0.046875 to 0.046875
- attend_output: bfloat16 [8192, 8192], P('tp', ('ctx', 'section')), may hold values from -0.0625 to 0.0625
Outputs:
- prompt_mixed: bfloat16 [8192, 16384], P(('ctx', 'section'), 'tp')
- decode_mixed: bfloat16 [128, 4, 8192], P('tp', None, ('ctx', 'section'))
The draws below stay inside these ranges and needn't reach their ends.
Inputs may be any that keep to these rules, and one draw needn't show every extreme that they name: `page_counts`: every row continues at least one page; some row continues all 16 pages and some row exactly one. `prompt_steps`: positive. `decode_steps`: positive.
All inputs are finite; a program needn't handle non-finite values.
Results may differ from the reference program's by a relative error of at most 0.02.
Values may be sent and summed in bfloat16 or wider, within the bound.
A program may use at most 320 MiB of HBM per device.

```python
import math
from functools import partial
import jax
import jax.numpy as jnp
from jax import lax

D = 8192
HEADS = 256
HEAD_DIM = 64
STATE = 256
GROUPS = 8
QHEADS = 64
KV_HEADS = 8
ATT_DIM = 128
TOK_DEV = 512
ROWS_DEV = 8
STEPS = 4
BLOCK = 256
SHARDS = 16
PROMPT = 8192
ROWS = 128


def head_scales(key, fast_share):
    first, second, third = jax.random.split(key, 3)
    fast = jax.random.uniform(first, (HEADS,)) < fast_share
    short_memory = jnp.exp(jax.random.uniform(second, (HEADS,), minval=math.log(30.0), maxval=math.log(50.0)))
    long_memory = PROMPT * jnp.exp(jax.random.uniform(third, (HEADS,), minval=0.0, maxval=math.log(4.0)))
    memory = jnp.where(fast, short_memory, long_memory)
    return memory ** (-0.5)


def shared_keys(key):
    return jnp.clip(jax.random.normal(key, (PROMPT, KV_HEADS * ATT_DIM), jnp.float32), -4.0, 4.0)


def draw_decay_logs(key, part):
    scales = head_scales(key, 0.5)
    return jnp.log(scales).astype(jnp.float32)


def draw_prompt_steps(key, part):
    scales = head_scales(key, 0.5)
    key = jax.random.fold_in(key, 2)
    first, second = jax.random.split(key)
    spread = jnp.exp(jax.random.uniform(first, (PROMPT, HEADS), minval=math.log(0.5), maxval=math.log(2.0)))
    factor = jnp.exp(jax.random.uniform(second, (SHARDS, 1, HEADS), minval=math.log(0.5), maxval=math.log(2.0)))
    factor = jnp.broadcast_to(factor, (SHARDS, TOK_DEV, HEADS)).reshape(PROMPT, HEADS)
    return (spread * factor * scales[None, :]).astype(jnp.float32)


def draw_decode_steps(key, part):
    scales = head_scales(key, 0.5)
    key = jax.random.fold_in(key, 3)
    spread = jnp.exp(jax.random.uniform(key, (ROWS, STEPS, HEADS), minval=math.log(0.5), maxval=math.log(2.0)))
    return (spread * scales).astype(jnp.float32)


def draw_page_counts(key, part):
    key = jax.random.fold_in(key, 4)
    counts = jax.random.randint(key, (ROWS,), 1, SHARDS + 1)
    owners = jnp.arange(SHARDS)
    leading = jnp.where(owners == 0, SHARDS, owners)
    counts = counts.at[owners * ROWS_DEV].set(leading)
    return counts.astype(jnp.int32)


def draw_prompt_keys(key, part):
    base = shared_keys(key)
    return base.astype(jnp.bfloat16)


def draw_decode_queries(key, part):
    key = jax.random.fold_in(key, 6)
    queries = jnp.clip(jax.random.normal(key, (ROWS, STEPS, QHEADS * ATT_DIM), jnp.float32), -4.0, 4.0)
    return queries.astype(jnp.bfloat16)


def levels(stream_key, shape, pieces, least, top_value):
    gain = 1.0
    for position, shards_of in pieces:
        heights = jax.random.uniform(jax.random.fold_in(jax.random.fold_in(stream_key, 6), position), (shards_of,), jnp.float32, least / len(pieces), top_value / len(pieces))
        gain = gain * jnp.repeat(jnp.exp(heights), shape[position] // shards_of).reshape((-1,) + (1,) * (len(shape) - 1 - position))
    return gain


def scatter_about(key, dims, scale, most, cuts=(), kind=jnp.bfloat16):
    array = scale * jax.random.normal(key, dims, jnp.float32)
    if cuts:
        array = array * levels(key, dims, cuts, -0.22, 0.18)
    return jnp.clip(array, -most, most).astype(kind)


def setup_inputs(seed: int = 0) -> dict:
    streams_of = jax.random.split(jax.random.key(seed), 22)
    return {
        "prompt_mixer": scatter_about(streams_of[0], (PROMPT, HEADS * HEAD_DIM), 1.0, 5.0, ((0, 16), (1, 8))),
        "prompt_gates": scatter_about(streams_of[1], (PROMPT, HEADS * HEAD_DIM), 1.0, 5.0, ((0, 16), (1, 8))),
        "prompt_write": scatter_about(streams_of[2], (PROMPT, GROUPS * STATE), 1.0, 5.0, ((0, 16), (1, 8))),
        "prompt_read": scatter_about(streams_of[3], (PROMPT, GROUPS * STATE), 0.0625, 1.0, ((0, 16), (1, 8))),
        "prompt_steps": draw_prompt_steps(jax.random.fold_in(streams_of[21], 71), 0),
        "decay_logs": draw_decay_logs(jax.random.fold_in(streams_of[21], 71), 0),
        "skip_weights": jnp.clip(0.5 + 1.0 * jax.random.uniform(streams_of[6], (HEADS,), jnp.float32) ** levels(streams_of[6], (HEADS,), ((0, 8),), -0.2, 0.2), 0.5, 1.5),
        "norm_gains": jnp.clip(1.0 + 0.18 * jax.random.normal(streams_of[7], (HEADS * HEAD_DIM,), jnp.float32), 0.1, 1.9),
        "prompt_keys": draw_prompt_keys(jax.random.fold_in(streams_of[21], 71), 0),
        "prompt_values": scatter_about(streams_of[9], (PROMPT, KV_HEADS * ATT_DIM), 1.0, 5.0, ((0, 16), (1, 8))),
        "page_counts": draw_page_counts(jax.random.fold_in(streams_of[21], 71), 0),
        "decode_mixer": scatter_about(streams_of[11], (ROWS, STEPS, HEADS * HEAD_DIM), 1.0, 5.0, ((0, 16), (2, 8))),
        "decode_gates": scatter_about(streams_of[12], (ROWS, STEPS, HEADS * HEAD_DIM), 1.0, 5.0, ((0, 16), (2, 8))),
        "decode_write": scatter_about(streams_of[13], (ROWS, STEPS, GROUPS * STATE), 1.0, 5.0, ((0, 16), (2, 8))),
        "decode_read": scatter_about(streams_of[14], (ROWS, STEPS, GROUPS * STATE), 0.0625, 1.0, ((0, 16), (2, 8))),
        "decode_steps": draw_decode_steps(jax.random.fold_in(streams_of[21], 71), 0),
        "decode_queries": draw_decode_queries(jax.random.fold_in(streams_of[21], 71), 0),
        "decode_keys": scatter_about(streams_of[17], (ROWS, STEPS, KV_HEADS * ATT_DIM), 1.0, 5.0, ((0, 16), (2, 8))),
        "decode_values": scatter_about(streams_of[18], (ROWS, STEPS, KV_HEADS * ATT_DIM), 1.0, 5.0, ((0, 16), (2, 8))),
        "mixer_output": scatter_about(streams_of[19], (HEADS * HEAD_DIM, D), (HEADS * HEAD_DIM) ** -0.5, 0.046875, ((0, 8), (1, 16))),
        "attend_output": scatter_about(streams_of[20], (QHEADS * ATT_DIM, D), (QHEADS * ATT_DIM) ** -0.5, 0.0625, ((0, 8), (1, 16))),
    }


HIGH = lax.Precision.HIGHEST
EPS = 1e-05

def ssd_block(decay_rate, per_group, carried, inputs):
    x_block, b_block, c_block, dt_block = inputs
    log_decay = jnp.cumsum(-dt_block * decay_rate, axis=0)
    block_len = x_block.shape[0]
    lower_mask = jnp.arange(block_len)[:, None] >= jnp.arange(block_len)[None, :]
    decay_gap = log_decay.T[:, :, None] - log_decay.T[:, None, :]
    lower_decay = jnp.where(lower_mask[None], jnp.exp(jnp.minimum(decay_gap, 0.0)), 0.0)
    affinity = jnp.einsum('qgn,kgn->gqk', c_block, b_block, precision=HIGH)
    affinity = jnp.repeat(affinity, per_group, axis=0)
    mixing = lower_decay * affinity * dt_block.T[:, None, :]
    out_block = jnp.einsum('hqk,khp->qhp', mixing, x_block, precision=HIGH)
    read_heads = jnp.repeat(c_block, per_group, axis=1)
    write_heads = jnp.repeat(b_block, per_group, axis=1)
    out_block = out_block + jnp.exp(log_decay)[:, :, None] * jnp.einsum('qhn,hpn->qhp', read_heads, carried, precision=HIGH)
    tail_weight = jnp.exp(log_decay[-1][None, :] - log_decay) * dt_block
    fresh_state = jnp.einsum('khp,khn->hpn', x_block * tail_weight[:, :, None], write_heads, precision=HIGH)
    carried = jnp.exp(log_decay[-1])[:, None, None] * carried + fresh_state
    return (carried, out_block)

def gated_norm(values, gates, gains, group_count):
    leading = values.shape[:-2]
    gated = values.reshape(leading + (-1,)) * jax.nn.silu(gates.astype(jnp.float32))
    grouped = gated.reshape(leading + (group_count, -1))
    scaled = grouped * lax.rsqrt(lax.optimization_barrier(jnp.mean(grouped * grouped, axis=-1, keepdims=True)) + EPS)
    return (scaled.reshape(leading + (-1,)) * gains).astype(jnp.bfloat16)

def reference(prompt_mixer, prompt_gates, prompt_write, prompt_read, prompt_steps, decay_logs, skip_weights, norm_gains, prompt_keys, prompt_values, page_counts, decode_mixer, decode_gates, decode_write, decode_read, decode_steps, decode_queries, decode_keys, decode_values, mixer_output, attend_output):
    per_group = HEADS // GROUPS
    blocks = TOK_DEV // BLOCK
    decay_rate = jnp.exp(decay_logs)
    mixer = prompt_mixer.astype(jnp.float32).reshape(SHARDS, blocks, BLOCK, HEADS, HEAD_DIM)
    write = prompt_write.astype(jnp.float32).reshape(SHARDS, blocks, BLOCK, GROUPS, STATE)
    read = prompt_read.astype(jnp.float32).reshape(SHARDS, blocks, BLOCK, GROUPS, STATE)
    steps = prompt_steps.reshape(SHARDS, blocks, BLOCK, HEADS)

    def shard_pass(carried, inputs):
        carried, outputs = lax.scan(partial(ssd_block, decay_rate, per_group), carried, inputs)
        return (carried, (outputs, carried))
    zero_state = jnp.zeros((HEADS, HEAD_DIM, STATE), jnp.float32)
    _, (outputs, shard_states) = lax.scan(shard_pass, zero_state, (mixer, write, read, steps))
    shard_states = lax.optimization_barrier(shard_states.astype(jnp.bfloat16)).astype(jnp.float32)
    mixer_flat = prompt_mixer.astype(jnp.float32).reshape(PROMPT, HEADS, HEAD_DIM)
    outputs = outputs.reshape(PROMPT, HEADS, HEAD_DIM) + skip_weights[None, :, None] * mixer_flat
    prompt_mixed = gated_norm(outputs, prompt_gates, norm_gains, GROUPS)
    keys_all = prompt_keys.astype(jnp.float32).reshape(PROMPT, KV_HEADS, ATT_DIM)
    values_all = prompt_values.astype(jnp.float32).reshape(PROMPT, KV_HEADS, ATT_DIM)
    group_size = QHEADS // KV_HEADS
    scale = ATT_DIM ** (-0.5)
    causal = jnp.arange(STEPS)[:, None] >= jnp.arange(STEPS)[None, :]

    def decode_row(inputs):
        count, mixer_row, gates_row, write_row, read_row, steps_row, query_row, key_row, value_row = inputs
        carried = lax.dynamic_index_in_dim(shard_states, (count - 1).astype(jnp.int32), keepdims=False)
        write_heads = jnp.repeat(write_row.astype(jnp.float32).reshape(STEPS, GROUPS, STATE), per_group, axis=1)
        read_heads = jnp.repeat(read_row.astype(jnp.float32).reshape(STEPS, GROUPS, STATE), per_group, axis=1)
        results = []
        for step_index in range(STEPS):
            mixer_now = mixer_row[step_index].astype(jnp.float32).reshape(HEADS, HEAD_DIM)
            dt_now = steps_row[step_index]
            carried = jnp.exp(-dt_now * decay_rate)[:, None, None] * carried + (dt_now[:, None] * mixer_now)[:, :, None] * write_heads[step_index][:, None, :]
            results.append(jnp.einsum('hn,hpn->hp', read_heads[step_index], carried, precision=HIGH) + skip_weights[:, None] * mixer_now)
        ssd_rows = gated_norm(jnp.stack(results), gates_row, norm_gains, GROUPS)
        queries = query_row.astype(jnp.float32).reshape(STEPS, KV_HEADS, group_size, ATT_DIM)
        own_keys = key_row.astype(jnp.float32).reshape(STEPS, KV_HEADS, ATT_DIM)
        own_values = value_row.astype(jnp.float32).reshape(STEPS, KV_HEADS, ATT_DIM)
        far_scores = jnp.einsum('skga,tka->skgt', queries, keys_all, precision=HIGH) * scale
        near_scores = jnp.einsum('skga,tka->skgt', queries, own_keys, precision=HIGH) * scale
        seen_far = (jnp.arange(PROMPT) < count * TOK_DEV)[None, None, None, :]
        seen_near = causal[:, None, None, :]
        far_scores = jnp.where(seen_far, far_scores, -1e+30)
        near_scores = jnp.where(seen_near, near_scores, -1e+30)
        top = jnp.maximum(lax.optimization_barrier(jnp.max(far_scores, axis=-1)), lax.optimization_barrier(jnp.max(near_scores, axis=-1)))
        far_weights = jnp.where(seen_far, jnp.exp(far_scores - top[..., None]), 0.0)
        near_weights = jnp.where(seen_near, jnp.exp(near_scores - top[..., None]), 0.0)
        total = lax.optimization_barrier(jnp.sum(far_weights, axis=-1)) + lax.optimization_barrier(jnp.sum(near_weights, axis=-1))
        far_round = lax.optimization_barrier(far_weights.astype(jnp.bfloat16)).astype(jnp.float32)
        near_round = lax.optimization_barrier(near_weights.astype(jnp.bfloat16)).astype(jnp.float32)
        summed = jnp.einsum('skgt,tka->skga', far_round, values_all, precision=HIGH)
        summed = summed + jnp.einsum('skgt,tka->skga', near_round, own_values, precision=HIGH)
        att_rows = (summed / total[..., None]).reshape(STEPS, QHEADS * ATT_DIM).astype(jnp.bfloat16)
        return (ssd_rows, att_rows)
    ssd_rows, att_rows = lax.map(decode_row, (page_counts, decode_mixer, decode_gates, decode_write, decode_read, decode_steps, decode_queries, decode_keys, decode_values))
    features = jnp.concatenate([ssd_rows, att_rows], axis=-1).reshape(ROWS * STEPS, -1)
    weight = jnp.concatenate([mixer_output, attend_output], axis=0)
    decode_mixed = jnp.dot(features, weight, preferred_element_type=jnp.float32).astype(jnp.bfloat16).reshape(ROWS, STEPS, D)
    return (prompt_mixed, decode_mixed)
```

```python
import jax
import jax.numpy as jnp
from jax import lax
from jax.experimental import pallas as pl
from jax.experimental.pallas import tpu as pltpu
from jax.sharding import PartitionSpec as P

HEADS, HEAD_DIM, STATE, GROUPS = 256, 64, 256, 8
QHEADS, KV_HEADS, ATT_DIM, STEPS = 64, 8, 128, 4
EPS = 1e-05
NEG = -1e30
F32, BF16 = jnp.float32, jnp.bfloat16
MESH = pl.DeviceIdType.MESH

PAGES = 16
TOK = 512
HL = 32
FEAT = HL * HEAD_DIM
ROWS = 8
RS = ROWS * STEPS
CH = 128
NCH = TOK // CH
QH = QHEADS // KV_HEADS
NQ = QH * RS
TILE = 256
NT = FEAT // TILE
COLS = 512
TP = 8
ALLF = FEAT + QH * ATT_DIM
SCALE = ATT_DIM ** -0.5


def dot(a, b):
    return jnp.dot(a, b, preferred_element_type=F32)


def dot_t(a, b):
    return lax.dot_general(a, b, (((1,), (1,)), ((), ())), preferred_element_type=F32)


def dot_tn(a, b):
    return lax.dot_general(a, b, (((0,), (0,)), ((), ())), preferred_element_type=F32)


def split2(v):
    hi = v.astype(BF16)
    return hi, (v - hi.astype(F32)).astype(BF16)


def split3(v):
    hi = v.astype(BF16)
    rest = v - hi.astype(F32)
    mid = rest.astype(BF16)
    return hi, mid, (rest - mid.astype(F32)).astype(BF16)


def place(p):
    return {"ctx": p // 2, "section": lax.rem(p, 2)}


def spot(x, z):
    return (z // 2) * 8 + x * 2 + lax.rem(z, 2)


def remote(src, dst, send, recv, device):
    return pltpu.make_async_remote_copy(
        src_ref=src, dst_ref=dst, send_sem=send, recv_sem=recv, device_id=device, device_id_type=MESH
    )


def kernel(
    x, gate, bm, cm, dt, dlog, skip, gains, keys, values, counts,
    xd, gd, bd, cd, dtd, qd, kd, vd, w1, w2,
    out, dec,
    kbuf, vbuf, qbuf, cbuf, s_send, s_recv, pst, e_recv, sc_send, sc_recv,
    o_send, o_recv, t_send, t_recv, feat, p_send, p_recv,
    exp_m, bt, mixg, a_hi, a_lo, b_hi, b_lo, small, rows, xp, chunk_s, yi, av, sq, fac,
    scores, acc, cntb, flat_x, flat_g, flat_b, flat_c, flat_dt, flat_q, flat_k, flat_v, ud,
    kv_ss, kv_rs, q_ss, q_rs, c_ss, c_rs, s_ss, s_rs, e_ss, e_rs, sc_ss, sc_rs,
    o_ss, o_rs, t_ss, t_rs, f1_ss, f1_rs, f2_ss, f2_rs, h1_ss, h1_rs, h2_ss, h2_rs, p_ss, p_rs,
):
    me = lax.axis_index("ctx") * 2 + lax.axis_index("section")
    tp = lax.axis_index("tp")
    xi = lax.rem(me // 2, 4)
    zi = (me // 8) * 2 + lax.rem(me, 2)

    def xpeer(d):
        return lax.rem(xi + d, 4)

    def zpeer(d):
        return lax.rem(zi + d, 4)

    barrier = pltpu.get_barrier_semaphore()

    def greet(d, c):
        pl.semaphore_signal(barrier, inc=1, device_id=place(lax.rem(me + d, PAGES)), device_id_type=MESH)
        return c

    def greet_tp(d, c):
        pl.semaphore_signal(barrier, inc=1, device_id={"tp": lax.rem(tp + d, TP)}, device_id_type=MESH)
        return c

    lax.fori_loop(1, PAGES, greet, 0)
    lax.fori_loop(1, TP, greet_tp, 0)

    for r in range(ROWS):
        sl = slice(r * STEPS, (r + 1) * STEPS)
        flat_q[sl, :] = qd[r].astype(F32)
        flat_c[sl, :] = cd[r].astype(F32)
    for h in range(QH):
        qbuf[xi, h * RS:(h + 1) * RS, :] = flat_q[:, h * ATT_DIM:(h + 1) * ATT_DIM].astype(BF16)
    cbuf[me] = flat_c[...].astype(BF16)

    pl.semaphore_wait(barrier, PAGES - 1 + TP - 1)

    kv_send, q_send = [], []
    for d in (1, 3, 2):
        dz = place(spot(xi, zpeer(d)))
        dx = place(spot(xpeer(d), zi))
        for i, (src, dst) in enumerate(((keys, kbuf), (values, vbuf))):
            cp = remote(src, dst.at[zi], kv_ss.at[i, d], kv_rs.at[i, d], dz)
            cp.start()
            kv_send.append(cp)
        cp = remote(qbuf.at[xi], qbuf.at[xi], q_ss.at[d], q_rs.at[d], dx)
        cp.start()
        q_send.append(cp)

    def c_copy(d, src):
        p = lax.rem(me + d, PAGES)
        return remote(cbuf.at[src], cbuf.at[src], c_ss.at[d], c_rs.at[d], place(p))

    def c_start(d, c):
        c_copy(d, me).start()
        return c

    lax.fori_loop(1, PAGES, c_start, 0)
    kbuf[zi] = keys[...]
    vbuf[zi] = values[...]

    row_i = lax.broadcasted_iota(jnp.int32, (CH, CH), 0)
    col_i = lax.broadcasted_iota(jnp.int32, (CH, CH), 1)
    lower = row_i >= col_i
    tri = lower.astype(F32).astype(BF16)
    head_of = lax.broadcasted_iota(jnp.int32, (HL, FEAT), 1) // HEAD_DIM
    exp_m[...] = (head_of == lax.broadcasted_iota(jnp.int32, (HL, FEAT), 0)).astype(F32).astype(BF16)
    rate = jnp.exp(dlog[...])
    base = jnp.zeros((1, HL), F32)
    for c in range(NCH):
        sl = slice(c * CH, (c + 1) * CH)
        step = dt[sl, :]
        hi, mid, lo = split3(-step * rate)
        log = dot(tri, hi) + dot(tri, mid) + dot(tri, lo)
        middle = log[CH // 2 - 1:CH // 2, :]
        last = log[CH - 1:CH, :]
        a_hi[sl, :], a_lo[sl, :] = split2(jnp.exp(log - middle))
        b_hi[sl, :], b_lo[sl, :] = split2(jnp.exp(middle - log) * step)
        small[c:c + 1, :] = jnp.exp(last)
        small[4 + c:5 + c, :] = jnp.exp(last - middle)
        small[8 + c:9 + c, :] = jnp.exp(middle)
        small[12 + c:13 + c, :] = jnp.exp(base + middle)
        base = base + last
        bt[c] = jnp.transpose(bm[sl, :].astype(F32)).astype(BF16)
    small[16:17, :] = jnp.exp(base)
    small[17:18, :] = skip[...]
    small[18:24, :] = jnp.zeros((6, HL), F32)
    hi, mid, lo = split3(small[...])
    rows[...] = dot(hi, exp_m[...]) + dot(mid, exp_m[...]) + dot(lo, exp_m[...])

    def states(nt, carry):
        ds = pl.ds(pl.multiple_of(nt * TILE, TILE), TILE)
        e = exp_m[:, ds]
        state = None
        for c in range(NCH):
            sl = slice(c * CH, (c + 1) * CH)
            w = dot(b_hi[sl, :], e) + dot(b_lo[sl, :], e)
            xs = (x[sl, ds].astype(F32) * w).astype(BF16)
            xp[sl, ds] = xs
            fresh = rows[4 + c:5 + c, ds] * dot(bt[c], xs)
            if c == 0:
                state = fresh
            else:
                chunk_s[c - 1, :, ds] = state.astype(BF16)
                state = rows[c:c + 1, ds] * state + fresh
        sent = state.astype(BF16)
        hi, mid, lo = split3(rows[16:17, ds])
        which = lax.broadcasted_iota(jnp.int32, (16, TILE), 0)
        tail = jnp.where(
            which == 0, hi.astype(F32), jnp.where(which == 1, mid.astype(F32), jnp.where(which == 2, lo.astype(F32), 0.0))
        ).astype(BF16)
        for half in range(2):
            hs = slice(half * 128, (half + 1) * 128)
            s_send[2 * nt + half, 0:STATE, :] = sent[:, hs]
            s_send[2 * nt + half, STATE:STATE + 16, :] = tail[:, hs]
        return carry

    lax.fori_loop(0, NT, states, 0)

    def s_copy(d, src, dst):
        p = lax.rem(me + d, PAGES)
        return remote(s_send.at[src], s_recv.at[dst], s_ss.at[d], s_rs.at[d], place(p))

    def s_start(d, c):
        s_copy(d, lax.rem(me + d, PAGES), me).start()
        return c

    lax.fori_loop(1, PAGES, s_start, 0)
    s_recv[me] = s_send[me]

    for d in (1, 3, 2):
        zsrc = zpeer(4 - d)
        for i, (src, dst) in enumerate(((keys, kbuf), (values, vbuf))):
            remote(src, dst.at[zsrc], kv_ss.at[i, d], kv_rs.at[i, d], place(spot(xi, zsrc))).wait_recv()
        xsrc = xpeer(4 - d)
        remote(qbuf.at[xsrc], qbuf.at[xsrc], q_ss.at[d], q_rs.at[d], place(spot(xsrc, zi))).wait_recv()

    token_of = lax.rem(lax.broadcasted_iota(jnp.int32, (1, NQ), 1), RS)
    row_of = token_of // STEPS

    def attend(i, carry):
        queries = qbuf[i]
        first = spot(i, zi) * ROWS
        seen = jnp.zeros((1, NQ), jnp.int32)
        for r in range(ROWS):
            seen = jnp.where(row_of == r, counts[first + r], seen)
        tops = []
        for z in range(4):
            bias = jnp.where(spot(xi, z) < seen, 0.0, NEG)
            for b in range(TOK // CH):
                s = dot_t(kbuf[z, b * CH:(b + 1) * CH, :], queries) + bias
                at = z * TOK + b * CH
                scores[at:at + CH, :] = s
                tops.append(jnp.max(s.reshape(CH // 8, 8, NQ), axis=0))
        while len(tops) > 1:
            tops = [jnp.maximum(p, q) for p, q in zip(tops[::2], tops[1::2])]
        top = jnp.max(tops[0], axis=0, keepdims=True)
        total = jnp.zeros((8, NQ), F32)
        summed = jnp.zeros((ATT_DIM, NQ), F32)
        for z in range(4):
            for b in range(TOK // CH):
                at = z * TOK + b * CH
                w = jnp.exp((scores[at:at + CH, :] - top) * SCALE)
                total = total + jnp.sum(w.reshape(CH // 8, 8, NQ), axis=0)
                summed = summed + dot_tn(vbuf[z, b * CH:(b + 1) * CH, :], w.astype(BF16))
        o_send[i] = summed.astype(BF16)
        which = lax.broadcasted_iota(jnp.int32, (8, NQ), 0)
        t_send[i] = jnp.where(which == 0, top, jnp.sum(total, axis=0, keepdims=True))
        return carry

    lax.fori_loop(0, 4, attend, 0)

    o_sent = []
    for d in (1, 3, 2):
        xp_d = xpeer(d)
        dx = place(spot(xp_d, zi))
        for src, dst, ss, rs in ((o_send, o_recv, o_ss, o_rs), (t_send, t_recv, t_ss, t_rs)):
            cp = remote(src.at[xp_d], dst.at[xi], ss.at[d], rs.at[d], dx)
            cp.start()
            o_sent.append(cp)
    o_recv[xi] = o_send[xi]
    t_recv[xi] = t_send[xi]

    for c in range(NCH):
        sl = slice(c * CH, (c + 1) * CH)
        mixg[c] = jnp.where(lower, dot_t(cm[sl, :], bm[sl, :]), 0.0).astype(BF16)

    def within(nt, carry):
        ds = pl.ds(pl.multiple_of(nt * TILE, TILE), TILE)
        e = exp_m[:, ds]
        for c in range(NCH):
            sl = slice(c * CH, (c + 1) * CH)
            y = dot(mixg[c], xp[sl, ds])
            if c > 0:
                y = y + rows[8 + c:9 + c, ds] * dot(cm[sl, :], chunk_s[c - 1, :, ds])
            a = dot(a_hi[sl, :], e) + dot(a_lo[sl, :], e)
            g = gate[sl, ds].astype(F32)
            g = g / (1.0 + jnp.exp(-g))
            yi[sl, ds] = g * (a * y + rows[17:18, ds] * x[sl, ds].astype(F32))
            av[sl, ds] = g * (a * rows[12 + c:13 + c, ds])
        return carry

    lax.fori_loop(0, NT, within, 0)

    for r in range(ROWS):
        sl = slice(r * STEPS, (r + 1) * STEPS)
        flat_k[sl, :] = kd[r].astype(F32)
        flat_v[sl, :] = vd[r].astype(F32)
        flat_x[sl, :] = xd[r].astype(F32)
        flat_g[sl, :] = gd[r].astype(F32)
        flat_b[sl, :] = bd[r].astype(F32)
        flat_dt[sl, :] = dtd[r]
    key_i = lax.broadcasted_iota(jnp.int32, (RS, NQ), 0)
    tok_i = lax.rem(lax.broadcasted_iota(jnp.int32, (RS, NQ), 1), RS)
    near_ok = jnp.logical_and(key_i // STEPS == tok_i // STEPS, key_i <= tok_i)
    near = jnp.where(near_ok, dot_t(flat_k[...].astype(BF16), qbuf[xi]), NEG)
    for d in (1, 3, 2):
        xsrc = xpeer(4 - d)
        dx = place(spot(xsrc, zi))
        remote(o_send.at[xsrc], o_recv.at[xsrc], o_ss.at[d], o_rs.at[d], dx).wait_recv()
        remote(t_send.at[xsrc], t_recv.at[xsrc], t_ss.at[d], t_rs.at[d], dx).wait_recv()
    top = jnp.max(near, axis=0, keepdims=True)
    for i in range(4):
        top = jnp.maximum(top, t_recv[i, 0:1, :])
    w = jnp.where(near_ok, jnp.exp((near - top) * SCALE), 0.0)
    total = jnp.sum(w, axis=0, keepdims=True)
    summed = dot_tn(flat_v[...].astype(BF16), w.astype(BF16))
    for i in range(4):
        part = jnp.exp((t_recv[i, 0:1, :] - top) * SCALE)
        total = total + part * t_recv[i, 1:2, :]
        summed = summed + part * o_recv[i].astype(F32)
    att = jnp.transpose(summed / total)
    for h in range(QH):
        feat[me, :, FEAT + h * ATT_DIM:FEAT + (h + 1) * ATT_DIM] = att[h * RS:(h + 1) * RS, :].astype(BF16)

    def gather(start, width, s1, r1, s2, r2):
        half = width // 2
        cols = (pl.ds(start, half), pl.ds(start + half, half))

        def peer(a, d):
            return spot(xi, zpeer(d)) if a == 0 else spot(xpeer(d), zi)

        def block(p, a):
            return feat.at[p, :, cols[a]]

        sent = []

        def go(p, a, send, recv, to):
            cp = remote(block(p, a), block(p, a), send, recv, place(to))
            cp.start()
            sent.append(cp)

        def forward(p, a, k):
            for d in (1, 3, 2):
                go(p, a, s2.at[a, k, d], r2.at[a, k, d], peer(1 - a, d))

        def first():
            for d in (1, 3, 2):
                for a in (0, 1):
                    go(me, a, s1.at[a, d], r1.at[a, d], peer(a, d))
            for a in (0, 1):
                forward(me, a, 0)

        def second():
            for d in (1, 3, 2):
                for a in (0, 1):
                    p = peer(a, 4 - d)
                    remote(block(p, a), block(p, a), s1.at[a, d], r1.at[a, d], place(p)).wait_recv()
                    forward(p, a, d)

        def finish():
            for k in (0, 1, 3, 2):
                for d in (1, 3, 2):
                    for a in (0, 1):
                        if a == 0:
                            p = spot(xpeer(4 - d), zpeer(4 - k))
                            q = spot(xpeer(4 - d), zi)
                        else:
                            p = spot(xpeer(4 - k), zpeer(4 - d))
                            q = spot(xi, zpeer(4 - d))
                        remote(block(p, a), block(p, a), s2.at[a, k, d], r2.at[a, k, d], place(q)).wait_recv()

        def drain():
            for cp in sent:
                cp.wait_send()

        return first, second, finish, drain

    h_first, h_second, h_finish, h_drain = gather(FEAT, ALLF - FEAT, h1_ss, h1_rs, h2_ss, h2_rs)
    f_first, f_second, f_finish, f_drain = gather(0, FEAT, f1_ss, f1_rs, f2_ss, f2_rs)
    h_first()

    def s_wait(d, c):
        src = lax.rem(me + PAGES - d, PAGES)
        s_copy(d, src, src).wait_recv()
        return c

    lax.fori_loop(1, PAGES, s_wait, 0)
    pst[0] = jnp.zeros((STATE, 128), BF16)

    def scan(k, state):
        tail = s_recv[k, STATE:STATE + 16, :].astype(F32)
        decay = tail[0:1, :] + tail[1:2, :] + tail[2:3, :]
        state = decay * state + s_recv[k, 0:STATE, :].astype(F32)
        pst[k + 1] = state.astype(BF16)
        return state

    lax.fori_loop(0, PAGES, scan, jnp.zeros((STATE, 128), F32))

    def c_wait(d, c):
        c_copy(d, lax.rem(me + PAGES - d, PAGES)).wait_recv()
        return c

    lax.fori_loop(1, PAGES, c_wait, 0)
    h_second()

    def fill(i, c):
        which = lax.broadcasted_iota(jnp.int32, (8, 128), 0)
        cntb[pl.ds(pl.multiple_of(i * 8, 8), 8), :] = jnp.where(which < 4, counts[2 * i], counts[2 * i + 1])
        return c

    lax.fori_loop(0, PAGES * ROWS // 2, fill, 0)

    for q in range(4):
        sl = slice(q * 128, (q + 1) * 128)
        reads = cbuf[q * 4:(q + 1) * 4].reshape(128, STATE)
        want = cntb[sl, :]

        def pick(k, got):
            return jnp.where(want == k, dot(reads, pst[k]), got)

        got = lax.fori_loop(1, PAGES + 1, pick, jnp.zeros((128, 128), F32))
        sc_send[q * 4:(q + 1) * 4] = got.astype(BF16).reshape(4, RS, 128)

    def sc_copy(d, src, dst):
        p = lax.rem(me + d, PAGES)
        return remote(sc_send.at[src], sc_recv.at[dst], sc_ss.at[d], sc_rs.at[d], place(p))

    def sc_start(d, c):
        sc_copy(d, lax.rem(me + d, PAGES), me).start()
        return c

    lax.fori_loop(1, PAGES, sc_start, 0)
    sc_recv[me] = sc_send[me]

    def e_copy(d, src, dst):
        p = lax.rem(me + d, PAGES)
        return remote(pst.at[src], e_recv.at[dst], e_ss.at[d], e_rs.at[d], place(p))

    def e_start(d, c):
        e_copy(d, lax.rem(me + d, PAGES), me).start()
        return c

    lax.fori_loop(1, PAGES, e_start, 0)
    e_recv[me] = pst[me]

    tok_r = lax.broadcasted_iota(jnp.int32, (RS, RS), 0)
    tok_c = lax.broadcasted_iota(jnp.int32, (RS, RS), 1)
    same = jnp.logical_and(tok_r // STEPS == tok_c // STEPS, tok_r >= tok_c)
    same_b = same.astype(F32).astype(BF16)
    hi, mid, lo = split3(-flat_dt[...] * rate)
    log = dot(same_b, hi) + dot(same_b, mid) + dot(same_b, lo)
    ad_hi, ad_lo = split2(jnp.exp(log))
    bd_hi, bd_lo = split2(jnp.exp(-log) * flat_dt[...])
    own = jnp.where(same, dot_t(flat_c[...].astype(BF16), flat_b[...].astype(BF16)), 0.0).astype(BF16)

    def sc_wait(d, c):
        src = lax.rem(me + PAGES - d, PAGES)
        sc_copy(d, src, src).wait_recv()
        return c

    lax.fori_loop(1, PAGES, sc_wait, 0)
    square = jnp.zeros((RS, TILE), F32)
    for nt in range(NT):
        ds = slice(nt * TILE, (nt + 1) * TILE)
        e = exp_m[:, ds]
        xt = flat_x[:, ds]
        ws = (xt * (dot(bd_hi, e) + dot(bd_lo, e))).astype(BF16)
        past = jnp.concatenate([sc_recv[2 * nt], sc_recv[2 * nt + 1]], axis=1).astype(F32)
        y = (dot(ad_hi, e) + dot(ad_lo, e)) * (dot(own, ws) + past) + rows[17:18, ds] * xt
        g = flat_g[:, ds]
        u = y * (g / (1.0 + jnp.exp(-g)))
        ud[:, ds] = u
        square = square + u * u
    scale = lax.rsqrt(jnp.sum(square, axis=1, keepdims=True) * (1.0 / FEAT) + EPS)
    feat[me, :, 0:FEAT] = (ud[...] * scale * gains[...]).astype(BF16)
    f_first()

    h_finish()

    def project_att(q, c):
        lhs = feat[pl.ds(q * 4, 4), :, FEAT:ALLF].reshape(128, ALLF - FEAT)
        acc[pl.ds(pl.multiple_of(q * 128, 128), 128), :] = dot(lhs, w2[...])
        return c

    lax.fori_loop(0, 4, project_att, 0)
    f_second()

    def e_wait(d, c):
        src = lax.rem(me + PAGES - d, PAGES)
        e_copy(d, src, src).wait_recv()
        return c

    lax.fori_loop(1, PAGES, e_wait, 0)
    sq[...] = jnp.zeros((TOK, 128), F32)

    def across(nt, carry):
        ds = pl.ds(pl.multiple_of(nt * TILE, TILE), TILE)
        entry = jnp.concatenate([e_recv[2 * nt], e_recv[2 * nt + 1]], axis=1)
        for c in range(NCH):
            sl = slice(c * CH, (c + 1) * CH)
            u = yi[sl, ds] + av[sl, ds] * dot(cm[sl, :], entry)
            yi[sl, ds] = u
            u2 = u * u
            sq[sl, :] = sq[sl, :] + u2[:, 0:128] + u2[:, 128:256]
        return carry

    lax.fori_loop(0, NT, across, 0)
    fac[...] = jnp.broadcast_to(
        lax.rsqrt(jnp.sum(sq[...], axis=1, keepdims=True) * (1.0 / FEAT) + EPS), (TOK, 128)
    )

    def normed(nt, carry):
        ds = pl.ds(pl.multiple_of(nt * 128, 128), 128)
        out[:, ds] = (yi[:, ds] * fac[...] * gains[:, ds]).astype(BF16)
        return carry

    lax.fori_loop(0, FEAT // 128, normed, 0)

    f_finish()
    for q in range(4):
        sl = slice(q * 128, (q + 1) * 128)
        lhs = feat[q * 4:(q + 1) * 4, :, 0:FEAT].reshape(128, FEAT)
        part = acc[sl, :] + dot(lhs, w1[...])
        acc[sl, :] = part
        p_send[2 * q:2 * q + 2] = part.astype(BF16).reshape(2, 64, COLS)

    def p_copy(d, src, dst):
        t = lax.rem(tp + d, TP)
        return remote(p_send.at[src], p_recv.at[dst], p_ss.at[d], p_rs.at[d], {"tp": t})

    def p_start(d, c):
        p_copy(d, lax.rem(tp + d, TP), tp).start()
        return c

    lax.fori_loop(1, TP, p_start, 0)
    mine = acc[pl.ds(pl.multiple_of(tp * 64, 64), 64), :]

    def p_sum(d, got):
        src = lax.rem(tp + TP - d, TP)
        p_copy(d, src, src).wait_recv()
        return got + p_recv[src].astype(F32)

    mine = lax.fori_loop(1, TP, p_sum, mine)
    for r in range(16):
        dec[r] = mine[r * STEPS:(r + 1) * STEPS, :].astype(BF16)

    for cp in kv_send + q_send + o_sent:
        cp.wait_send()
    h_drain()
    f_drain()

    def drain(d, c):
        p = lax.rem(me + d, PAGES)
        c_copy(d, me).wait_send()
        s_copy(d, p, me).wait_send()
        sc_copy(d, p, me).wait_send()
        e_copy(d, p, me).wait_send()
        return c

    lax.fori_loop(1, PAGES, drain, 0)

    def drain_tp(d, c):
        p_copy(d, lax.rem(tp + d, TP), tp).wait_send()
        return c

    lax.fori_loop(1, TP, drain_tp, 0)


def on_device(
    prompt_mixer, prompt_gates, prompt_write, prompt_read, prompt_steps, decay_logs, skip_weights, norm_gains,
    prompt_keys, prompt_values, page_counts, decode_mixer, decode_gates, decode_write, decode_read, decode_steps,
    decode_queries, decode_keys, decode_values, mixer_output, attend_output,
):
    vmem = pl.BlockSpec(memory_space=pltpu.VMEM)
    smem = pl.BlockSpec(memory_space=pltpu.SMEM)
    v = pltpu.VMEM
    dma = pltpu.SemaphoreType.DMA
    scratch = [
        v((4, TOK, ATT_DIM), BF16), v((4, TOK, ATT_DIM), BF16), v((4, NQ, ATT_DIM), BF16),
        v((PAGES, RS, STATE), BF16),
        v((PAGES, STATE + 16, 128), BF16), v((PAGES, STATE + 16, 128), BF16),
        v((PAGES + 1, STATE, 128), BF16), v((PAGES, STATE, 128), BF16),
        v((PAGES, RS, 128), BF16), v((PAGES, RS, 128), BF16),
        v((4, ATT_DIM, NQ), BF16), v((4, ATT_DIM, NQ), BF16), v((4, 8, NQ), F32), v((4, 8, NQ), F32),
        v((PAGES, RS, ALLF), BF16), v((TP, 64, COLS), BF16), v((TP, 64, COLS), BF16),
        v((HL, FEAT), BF16), v((NCH, STATE, CH), BF16), v((NCH, CH, CH), BF16),
        v((TOK, HL), BF16), v((TOK, HL), BF16), v((TOK, HL), BF16), v((TOK, HL), BF16),
        v((24, HL), F32), v((24, FEAT), F32), v((TOK, FEAT), BF16), v((NCH - 1, STATE, FEAT), BF16),
        v((TOK, FEAT), F32), v((TOK, FEAT), F32), v((TOK, 128), F32), v((TOK, 128), F32),
        v((4 * TOK, NQ), F32), v((PAGES * RS, COLS), F32), v((PAGES * RS, 128), jnp.int32),
        v((RS, FEAT), F32), v((RS, FEAT), F32), v((RS, STATE), F32), v((RS, STATE), F32), v((RS, HL), F32),
        v((RS, QH * ATT_DIM), F32), v((RS, ATT_DIM), F32), v((RS, ATT_DIM), F32), v((RS, FEAT), F32),
        dma((2, 4)), dma((2, 4)), dma((4,)), dma((4,)), dma((PAGES,)), dma((PAGES,)),
        dma((PAGES,)), dma((PAGES,)), dma((PAGES,)), dma((PAGES,)), dma((PAGES,)), dma((PAGES,)),
        dma((4,)), dma((4,)), dma((4,)), dma((4,)),
        dma((2, 4)), dma((2, 4)), dma((2, 4, 4)), dma((2, 4, 4)),
        dma((2, 4)), dma((2, 4)), dma((2, 4, 4)), dma((2, 4, 4)),
        dma((TP,)), dma((TP,)),
    ]
    specs = [vmem] * 10 + [smem] + [vmem] * 10
    return pl.pallas_call(
        kernel,
        out_shape=(
            jax.ShapeDtypeStruct((TOK, FEAT), BF16),
            jax.ShapeDtypeStruct((16, STEPS, COLS), BF16),
        ),
        in_specs=specs,
        out_specs=(vmem, vmem),
        scratch_shapes=scratch,
        compiler_params=pltpu.CompilerParams(
            collective_id=0, has_side_effects=True, vmem_limit_bytes=60 * 2**20
        ),
        name="layers",
    )(
        prompt_mixer, prompt_gates, prompt_write, prompt_read, prompt_steps,
        decay_logs.reshape(1, HL), skip_weights.reshape(1, HL), norm_gains.reshape(1, FEAT),
        prompt_keys, prompt_values, page_counts,
        decode_mixer, decode_gates, decode_write, decode_read, decode_steps,
        decode_queries, decode_keys, decode_values, mixer_output, attend_output,
    )


def solution(mesh):
    rows, heads = ("ctx", "section"), "tp"
    split = P(rows, heads)
    split3d = P(rows, None, heads)
    return jax.shard_map(
        on_device,
        mesh=mesh,
        in_specs=(split,) * 5 + (P(heads),) * 3 + (split,) * 2 + (P(),) + (split3d,) * 8 + (P(heads, rows),) * 2,
        out_specs=(split, P(heads, None, rows)),
        check_vma=False,
    )
```

```python
import jax
import jax.numpy as jnp
from jax import lax
from jax.experimental import pallas as pl
from jax.experimental.pallas import tpu as pltpu
from jax.sharding import PartitionSpec as P

HEADS, HEAD_DIM, STATE, GROUPS = 256, 64, 256, 8
QHEADS, KV_HEADS, ATT_DIM, STEPS = 64, 8, 128, 4
EPS = 1e-05
OFFSETS = ((2, 2), (1, 0), (0, 1), (3, 0), (0, 3), (2, 1), (1, 2), (2, 3), (3, 2), (1, 1), (3, 3), (1, 3), (3, 1), (2, 0), (0, 2))
MID = 15
NEG = -1e30
F32, BF16 = jnp.float32, jnp.bfloat16
MESH = pl.DeviceIdType.MESH

PAGES = 16
TOK = 512
HL = 32
FEAT = HL * HEAD_DIM
ROWS = 8
RS = ROWS * STEPS
CH = 128
NCH = TOK // CH
QH = QHEADS // KV_HEADS
NQ = QH * RS
TILE = 256
NT = FEAT // TILE
COLS = 512
TP = 8
ALLF = FEAT + QH * ATT_DIM
SCALE = ATT_DIM ** -0.5


def dot(a, b):
    return jnp.dot(a, b, preferred_element_type=F32)


def dot_t(a, b):
    return lax.dot_general(a, b, (((1,), (1,)), ((), ())), preferred_element_type=F32)


def dot_tn(a, b):
    return lax.dot_general(a, b, (((0,), (0,)), ((), ())), preferred_element_type=F32)


def split2(v):
    hi = v.astype(BF16)
    return hi, (v - hi.astype(F32)).astype(BF16)


def stack2(v):
    hi = v.astype(BF16).astype(F32)
    return jnp.concatenate([hi, v - hi], axis=1).astype(BF16)


def split3(v):
    hi = v.astype(BF16)
    rest = v - hi.astype(F32)
    mid = rest.astype(BF16)
    return hi, mid, (rest - mid.astype(F32)).astype(BF16)


def place(p):
    return {"ctx": p // 2, "section": lax.rem(p, 2)}


def spot(x, z):
    return (z // 2) * 8 + x * 2 + lax.rem(z, 2)


def remote(src, dst, send, recv, device):
    return pltpu.make_async_remote_copy(
        src_ref=src, dst_ref=dst, send_sem=send, recv_sem=recv, device_id=device, device_id_type=MESH
    )


def kernel(
    x_hbm, gate_hbm, bm, cm, dt_t, dlog, skip, gains, keys, values, counts,
    xd, gd, bd, cd, dtd, qd, kd, vd, w1_hbm, w2_hbm,
    out_hbm, dec,
    x, gate, w1, w2, out, in_sem, out_sem,
    kbuf, vbuf, qbuf, cbuf, s_send, s_recv, pst, e_recv, sc_send, sc_recv,
    o_send, o_recv, t_send, t_recv, feat, p_send, p_recv,
    exp_m, bt, mixg, a_w, b_w, end_w, small, rows, yi, av, sq, fac,
    scores, acc, cntb, picked, flat_x, flat_g, flat_b, flat_c, flat_dt, flat_q, flat_k, flat_v, ud,
    kv_ss, kv_rs, q_ss, q_rs, c_ss, c_rs, s_ss, s_rs, e_ss, e_rs, sc_ss, sc_rs,
    o_ss, o_rs, t_ss, t_rs, f1_ss, f1_rs, f2_ss, f2_rs, h1_ss, h1_rs, h2_ss, h2_rs, p_ss, p_rs,
):
    me = lax.axis_index("ctx") * 2 + lax.axis_index("section")
    tp = lax.axis_index("tp")
    xi = lax.rem(me // 2, 4)
    zi = (me // 8) * 2 + lax.rem(me, 2)

    def xpeer(d):
        return lax.rem(xi + d, 4)

    def zpeer(d):
        return lax.rem(zi + d, 4)

    barrier = pltpu.get_barrier_semaphore()

    class Peer:
        def __init__(self, n, dx, dz):
            self.n = n
            self.to = spot(xpeer(dx), zpeer(dz))
            self.to_place = place(self.to)
            self.back = spot(xpeer(4 - dx), zpeer(4 - dz))

    peers = [Peer(n, dx, dz) for n, (dx, dz) in enumerate(OFFSETS)]
    for peer in peers:
        pl.semaphore_signal(barrier, inc=1, device_id=peer.to_place, device_id_type=MESH)
    tpeers = [lax.rem(tp + d, TP) for d in range(1, TP)]
    for t in tpeers:
        pl.semaphore_signal(barrier, inc=1, device_id={"tp": t}, device_id_type=MESH)

    loads = [
        pltpu.make_async_copy(src, dst, in_sem.at[i])
        for i, (src, dst) in enumerate(((x_hbm, x), (gate_hbm, gate), (w2_hbm, w2), (w1_hbm, w1)))
    ]
    for cp in loads:
        cp.start()

    for r in range(ROWS):
        sl = slice(r * STEPS, (r + 1) * STEPS)
        flat_q[sl, :] = qd[r].astype(F32)
        flat_c[sl, :] = cd[r].astype(F32)
    for h in range(QH):
        qbuf[xi, h * RS:(h + 1) * RS, :] = flat_q[:, h * ATT_DIM:(h + 1) * ATT_DIM].astype(BF16)
    cbuf[me] = flat_c[...].astype(BF16)

    row_i = lax.broadcasted_iota(jnp.int32, (CH, CH), 0)
    col_i = lax.broadcasted_iota(jnp.int32, (CH, CH), 1)
    lower = row_i >= col_i
    tri = lower.astype(F32).astype(BF16)
    head_of = lax.broadcasted_iota(jnp.int32, (2 * HL, FEAT), 1) // HEAD_DIM
    head_is = lax.rem(lax.broadcasted_iota(jnp.int32, (2 * HL, FEAT), 0), HL)
    exp_m[...] = (head_of == head_is).astype(F32).astype(BF16)
    rate = jnp.exp(dlog[...])
    base = jnp.zeros((1, HL), F32)
    logs, steps = [], []
    for c in range(NCH):
        sl = slice(c * CH, (c + 1) * CH)
        step = jnp.transpose(dt_t[:, sl])
        hi, mid, lo = split3(-step * rate)
        log = dot(tri, hi) + dot(tri, mid) + dot(tri, lo)
        middle = log[CH // 2 - 1:CH // 2, :]
        last = log[CH - 1:CH, :]
        logs.append(base + log)
        steps.append(step)
        a_w[sl, :] = stack2(jnp.exp(log - middle))
        b_w[sl, :] = stack2(jnp.exp(middle - log) * step)
        small[c:c + 1, :] = jnp.exp(last)
        small[4 + c:5 + c, :] = jnp.exp(last - middle)
        small[8 + c:9 + c, :] = jnp.exp(middle)
        small[12 + c:13 + c, :] = jnp.exp(base + middle)
        base = base + last
    for c in range(NCH):
        sl = slice(c * CH, (c + 1) * CH)
        end_w[sl, :] = stack2(jnp.exp(base - logs[c]) * steps[c])
        bt[:, sl] = jnp.transpose(bm[sl, :].astype(F32)).astype(BF16)
    small[16:17, :] = jnp.exp(base)
    small[17:18, :] = skip[...]
    small[18:24, :] = jnp.zeros((6, HL), F32)
    hi, mid, lo = split3(small[...])
    one = exp_m[0:HL, :]
    rows[...] = dot(hi, one) + dot(mid, one) + dot(lo, one)

    pl.semaphore_wait(barrier, PAGES - 1 + TP - 1)

    up, down = spot(xi, zpeer(1)), spot(xi, zpeer(3))
    kv_send, q_send = [], []

    def kv(buf, n, block, to, i):
        return remote(block, buf.at[n], kv_ss.at[i], kv_rs.at[i], place(to))

    for i, (src, buf) in enumerate(((keys, kbuf), (values, vbuf))):
        for k, to in ((0, up), (1, down)):
            cp = kv(buf, zi, src, to, 2 * i + k)
            cp.start()
            kv_send.append(cp)
    for d in (1, 3, 2):
        cp = remote(qbuf.at[xi], qbuf.at[xi], q_ss.at[d], q_rs.at[d], place(spot(xpeer(d), zi)))
        cp.start()
        q_send.append(cp)
    kbuf[zi] = keys[...]
    vbuf[zi] = values[...]

    loads[0].wait()

    def states(nt, carry):
        ds = pl.ds(pl.multiple_of(nt * TILE, TILE), TILE)
        e = exp_m[:, ds]
        xs = (x[:, ds].astype(F32) * dot(end_w[...], e)).astype(BF16)
        state = dot(bt[...], xs)
        sent = state.astype(BF16)
        hi, mid, lo = split3(rows[16:17, ds])
        which = lax.broadcasted_iota(jnp.int32, (16, TILE), 0)
        tail = jnp.where(
            which == 0, hi.astype(F32), jnp.where(which == 1, mid.astype(F32), jnp.where(which == 2, lo.astype(F32), 0.0))
        ).astype(BF16)
        for half in range(2):
            hs = slice(half * 128, (half + 1) * 128)
            s_send[2 * nt + half, 0:STATE, :] = sent[:, hs]
            s_send[2 * nt + half, STATE:STATE + 16, :] = tail[:, hs]
        return carry

    lax.fori_loop(0, NT, states, 0)

    kv(kbuf, zpeer(3), keys, up, 0).wait_recv()
    cp = kv(kbuf, zpeer(3), kbuf.at[zpeer(3)], up, 4)
    cp.start()
    kv_send.append(cp)
    kv(vbuf, zpeer(1), values, down, 3).wait_recv()
    cp = kv(vbuf, zpeer(1), vbuf.at[zpeer(1)], down, 5)
    cp.start()
    kv_send.append(cp)

    def exchange(src, dst, send, recv):
        def copy(peer):
            return remote(src.at[peer.to], dst.at[me], send.at[peer.n], recv.at[peer.n], peer.to_place)

        def landed(peer):
            remote(src.at[peer.back], dst.at[peer.back], send.at[peer.n], recv.at[peer.n], place(peer.back)).wait_recv()

        return copy, landed

    s_copy, s_landed = exchange(s_send, s_recv, s_ss, s_rs)
    sc_copy, sc_landed = exchange(sc_send, sc_recv, sc_ss, sc_rs)
    e_copy, e_landed = exchange(pst, e_recv, e_ss, e_rs)

    def c_copy(peer, src):
        return remote(cbuf.at[src], cbuf.at[src], c_ss.at[peer.n], c_rs.at[peer.n], peer.to_place)

    for peer in peers:
        s_copy(peer).start()
    for peer in peers:
        c_copy(peer, me).start()
    s_recv[me] = s_send[me]

    kv(kbuf, zpeer(1), keys, down, 1).wait_recv()
    kv(vbuf, zpeer(3), values, up, 2).wait_recv()
    kv(kbuf, zpeer(2), keys, up, 4).wait_recv()
    kv(vbuf, zpeer(2), values, down, 5).wait_recv()
    for d in (1, 3, 2):
        xsrc = xpeer(4 - d)
        remote(qbuf.at[xsrc], qbuf.at[xsrc], q_ss.at[d], q_rs.at[d], place(spot(xsrc, zi))).wait_recv()

    token_of = lax.rem(lax.broadcasted_iota(jnp.int32, (1, NQ), 1), RS)
    row_of = token_of // STEPS

    def attend(i, carry):
        queries = qbuf[i]
        first = spot(i, zi) * ROWS
        seen = jnp.zeros((1, NQ), jnp.int32)
        for r in range(ROWS):
            seen = jnp.where(row_of == r, counts[first + r], seen)
        tops = []
        for z in range(4):
            bias = jnp.where(spot(xi, z) < seen, 0.0, NEG)
            for b in range(TOK // CH):
                s = dot_t(kbuf[z, b * CH:(b + 1) * CH, :], queries) + bias
                at = z * TOK + b * CH
                scores[at:at + CH, :] = s
                tops.append(jnp.max(s.reshape(CH // 8, 8, NQ), axis=0))
        while len(tops) > 1:
            tops = [jnp.maximum(p, q) for p, q in zip(tops[::2], tops[1::2])]
        top = jnp.max(tops[0], axis=0, keepdims=True)
        total = jnp.zeros((8, NQ), F32)
        summed = jnp.zeros((ATT_DIM, NQ), F32)
        for z in range(4):
            for b in range(TOK // CH):
                at = z * TOK + b * CH
                w = jnp.exp((scores[at:at + CH, :] - top) * SCALE)
                total = total + jnp.sum(w.reshape(CH // 8, 8, NQ), axis=0)
                summed = summed + dot_tn(vbuf[z, b * CH:(b + 1) * CH, :], w.astype(BF16))
        o_send[i] = summed.astype(BF16)
        which = lax.broadcasted_iota(jnp.int32, (8, NQ), 0)
        t_send[i] = jnp.where(which == 0, top, jnp.sum(total, axis=0, keepdims=True))
        return carry

    lax.fori_loop(0, 4, attend, 0)

    o_sent = []
    for d in (1, 3, 2):
        xp_d = xpeer(d)
        dx = place(spot(xp_d, zi))
        for src, dst, ss, rs in ((o_send, o_recv, o_ss, o_rs), (t_send, t_recv, t_ss, t_rs)):
            cp = remote(src.at[xp_d], dst.at[xi], ss.at[d], rs.at[d], dx)
            cp.start()
            o_sent.append(cp)
    o_recv[xi] = o_send[xi]
    t_recv[xi] = t_send[xi]

    for peer in peers:
        c_copy(peer, peer.back).wait_recv()

    def fill(i, c):
        which = lax.broadcasted_iota(jnp.int32, (8, 128), 0)
        cntb[pl.ds(pl.multiple_of(i * 8, 8), 8), :] = jnp.where(which < 4, counts[2 * i], counts[2 * i + 1])
        return c

    lax.fori_loop(0, PAGES * ROWS // 2, fill, 0)

    def mask_reads(k, c):
        for q in range(4):
            sl = slice(q * 128, (q + 1) * 128)
            reads = cbuf[q * 4:(q + 1) * 4].reshape(128, STATE).astype(F32)
            want = cntb[sl, :] == k + 1
            for half in range(2):
                hs = slice(half * 128, (half + 1) * 128)
                at = pl.ds(pl.multiple_of(k * STATE + half * 128, 128), 128)
                picked[sl, at] = jnp.where(want, reads[:, hs], 0.0).astype(BF16)
        return c

    lax.fori_loop(0, PAGES, mask_reads, 0)

    for r in range(ROWS):
        sl = slice(r * STEPS, (r + 1) * STEPS)
        flat_k[sl, :] = kd[r].astype(F32)
        flat_v[sl, :] = vd[r].astype(F32)
        flat_x[sl, :] = xd[r].astype(F32)
        flat_g[sl, :] = gd[r].astype(F32)
        flat_b[sl, :] = bd[r].astype(F32)
        flat_dt[sl, :] = dtd[r]
    key_i = lax.broadcasted_iota(jnp.int32, (RS, NQ), 0)
    tok_i = lax.rem(lax.broadcasted_iota(jnp.int32, (RS, NQ), 1), RS)
    near_ok = jnp.logical_and(key_i // STEPS == tok_i // STEPS, key_i <= tok_i)
    near = jnp.where(near_ok, dot_t(flat_k[...].astype(BF16), qbuf[xi]), NEG)
    for d in (1, 3, 2):
        xsrc = xpeer(4 - d)
        dx = place(spot(xsrc, zi))
        remote(o_send.at[xsrc], o_recv.at[xsrc], o_ss.at[d], o_rs.at[d], dx).wait_recv()
        remote(t_send.at[xsrc], t_recv.at[xsrc], t_ss.at[d], t_rs.at[d], dx).wait_recv()
    top = jnp.max(near, axis=0, keepdims=True)
    for i in range(4):
        top = jnp.maximum(top, t_recv[i, 0:1, :])
    w = jnp.where(near_ok, jnp.exp((near - top) * SCALE), 0.0)
    total = jnp.sum(w, axis=0, keepdims=True)
    summed = dot_tn(flat_v[...].astype(BF16), w.astype(BF16))
    for i in range(4):
        part = jnp.exp((t_recv[i, 0:1, :] - top) * SCALE)
        total = total + part * t_recv[i, 1:2, :]
        summed = summed + part * o_recv[i].astype(F32)
    att = jnp.transpose(summed / total)
    for h in range(QH):
        feat[me, :, FEAT + h * ATT_DIM:FEAT + (h + 1) * ATT_DIM] = att[h * RS:(h + 1) * RS, :].astype(BF16)

    def gather(start, width, s1, r1, s2, r2):
        half = width // 2
        cols = (pl.ds(start, half), pl.ds(start + half, half))

        def peer(a, d):
            return spot(xi, zpeer(d)) if a == 0 else spot(xpeer(d), zi)

        def block(p, a):
            return feat.at[p, :, cols[a]]

        sent = []

        def go(p, a, send, recv, to):
            cp = remote(block(p, a), block(p, a), send, recv, place(to))
            cp.start()
            sent.append(cp)

        def forward(p, a, k):
            for d in (1, 3, 2):
                go(p, a, s2.at[a, k, d], r2.at[a, k, d], peer(1 - a, d))

        def first():
            for d in (1, 3, 2):
                for a in (0, 1):
                    go(me, a, s1.at[a, d], r1.at[a, d], peer(a, d))
            for a in (0, 1):
                forward(me, a, 0)

        def second():
            for d in (1, 3, 2):
                for a in (0, 1):
                    p = peer(a, 4 - d)
                    remote(block(p, a), block(p, a), s1.at[a, d], r1.at[a, d], place(p)).wait_recv()
                    forward(p, a, d)

        def finish():
            for k in (0, 1, 3, 2):
                for d in (1, 3, 2):
                    for a in (0, 1):
                        if a == 0:
                            p = spot(xpeer(4 - d), zpeer(4 - k))
                            q = spot(xpeer(4 - d), zi)
                        else:
                            p = spot(xpeer(4 - k), zpeer(4 - d))
                            q = spot(xi, zpeer(4 - d))
                        remote(block(p, a), block(p, a), s2.at[a, k, d], r2.at[a, k, d], place(q)).wait_recv()

        def drain():
            for cp in sent:
                cp.wait_send()

        return first, second, finish, drain

    h_first, h_second, h_finish, h_drain = gather(FEAT, ALLF - FEAT, h1_ss, h1_rs, h2_ss, h2_rs)
    f_first, f_second, f_finish, f_drain = gather(0, FEAT, f1_ss, f1_rs, f2_ss, f2_rs)
    h_first()

    tok_r = lax.broadcasted_iota(jnp.int32, (RS, RS), 0)
    tok_c = lax.broadcasted_iota(jnp.int32, (RS, RS), 1)
    same = jnp.logical_and(tok_r // STEPS == tok_c // STEPS, tok_r >= tok_c)
    same_b = same.astype(F32).astype(BF16)
    hi, mid, lo = split3(-flat_dt[...] * rate)
    log = dot(same_b, hi) + dot(same_b, mid) + dot(same_b, lo)
    ad_w = stack2(jnp.exp(log))
    bd_w = stack2(jnp.exp(-log) * flat_dt[...])
    own = jnp.where(same, dot_t(flat_c[...].astype(BF16), flat_b[...].astype(BF16)), 0.0).astype(BF16)

    for nt in range(NT):
        ds = slice(nt * TILE, (nt + 1) * TILE)
        e = exp_m[:, ds]
        xt = flat_x[:, ds]
        ws = (xt * dot(bd_w, e)).astype(BF16)
        g = flat_g[:, ds]
        g = g / (1.0 + jnp.exp(-g))
        a = dot(ad_w, e)
        ud[:, ds] = g * (a * dot(own, ws) + rows[17:18, ds] * xt)
        flat_g[:, ds] = g * a

    for peer in peers:
        s_landed(peer)
    pst[0] = jnp.zeros((STATE, 128), BF16)

    def scan(k, state):
        tail = s_recv[k, STATE:STATE + 16, :].astype(F32)
        decay = tail[0:1, :] + tail[1:2, :] + tail[2:3, :]
        state = decay * state + s_recv[k, 0:STATE, :].astype(F32)
        pst[k + 1] = state.astype(BF16)
        return state

    lax.fori_loop(0, PAGES, scan, jnp.zeros((STATE, 128), F32), unroll=4)

    for q in range(2):
        sl = slice(q * 256, (q + 1) * 256)
        got = dot(picked[sl, :], pst[1:PAGES + 1].reshape(PAGES * STATE, 128))
        sc_send[q * 8:(q + 1) * 8] = got.astype(BF16).reshape(8, RS, 128)

    for peer in peers:
        sc_copy(peer).start()
    sc_recv[me] = sc_send[me]

    h_second()
    e_recv[me] = pst[me]

    for peer in peers:
        sc_landed(peer)
    square = jnp.zeros((RS, TILE), F32)
    for nt in range(NT):
        ds = slice(nt * TILE, (nt + 1) * TILE)
        past = jnp.concatenate([sc_recv[2 * nt], sc_recv[2 * nt + 1]], axis=1).astype(F32)
        u = ud[:, ds] + flat_g[:, ds] * past
        ud[:, ds] = u
        square = square + u * u
    scale = lax.rsqrt(jnp.sum(square, axis=1, keepdims=True) * (1.0 / FEAT) + EPS)
    feat[me, :, 0:FEAT] = (ud[...] * scale * gains[...]).astype(BF16)
    f_first()

    loads[1].wait()
    for c in range(NCH):
        sl = slice(c * CH, (c + 1) * CH)
        mixg[c] = jnp.where(lower, dot_t(cm[sl, :], bm[sl, :]), 0.0).astype(BF16)

    def within(nt, carry):
        ds = pl.ds(pl.multiple_of(nt * TILE, TILE), TILE)
        e = exp_m[:, ds]
        state = None
        for c in range(NCH):
            sl = slice(c * CH, (c + 1) * CH)
            xf = x[sl, ds].astype(F32)
            xs = (xf * dot(b_w[sl, :], e)).astype(BF16)
            y = dot(mixg[c], xs)
            if c > 0:
                y = y + rows[8 + c:9 + c, ds] * dot(cm[sl, :], state.astype(BF16))
            if c < NCH - 1:
                fresh = rows[4 + c:5 + c, ds] * dot(bt[:, sl], xs)
                state = fresh if c == 0 else rows[c:c + 1, ds] * state + fresh
            a = dot(a_w[sl, :], e)
            g = gate[sl, ds].astype(F32)
            g = g / (1.0 + jnp.exp(-g))
            yi[sl, ds] = g * (a * y + rows[17:18, ds] * xf)
            av[sl, ds] = g * (a * rows[12 + c:13 + c, ds])
        return carry

    lax.fori_loop(0, NT // 2, within, 0)
    f_second()
    for peer in peers[:MID]:
        e_copy(peer).start()
    lax.fori_loop(NT // 2, NT, within, 0)

    h_finish()
    loads[2].wait()

    def project_att(q, c):
        lhs = feat[pl.ds(q * 4, 4), :, FEAT:ALLF].reshape(128, ALLF - FEAT)
        acc[pl.ds(pl.multiple_of(q * 128, 128), 128), :] = dot(lhs, w2[...])
        return c

    lax.fori_loop(0, 4, project_att, 0)
    loads[3].wait()

    f_finish()

    def p_copy(d, src, dst):
        t = lax.rem(tp + d, TP)
        return remote(p_send.at[src], p_recv.at[dst], p_ss.at[d], p_rs.at[d], {"tp": t})

    for turn in (1, 3, 2, 0):
        q = lax.rem(tp // 2 + turn, 4)
        at = pl.ds(pl.multiple_of(q * 128, 128), 128)
        lhs = feat[pl.ds(q * 4, 4), :, 0:FEAT].reshape(128, FEAT)
        part = acc[at, :] + dot(lhs, w1[...])
        if turn == 0:
            acc[at, :] = part
        p_send[pl.ds(2 * q, 2)] = part.astype(BF16).reshape(2, 64, COLS)
        for half in range(2):
            t = 2 * q + half
            d = lax.rem(t - tp + TP, TP)
            if turn == 0:
                @pl.when(d != 0)
                def _():
                    p_copy(d, t, tp).start()
            else:
                p_copy(d, t, tp).start()

    for peer in peers[MID:]:
        e_copy(peer).start()
    sq[...] = jnp.zeros((TOK, 128), F32)
    for n in range(PAGES):
        if n > 0:
            e_landed(peers[n - 1])
        src = me if n == 0 else peers[n - 1].back
        ds = pl.ds(pl.multiple_of(src * 128, 128), 128)
        entry = e_recv[src]
        for c in range(NCH):
            sl = slice(c * CH, (c + 1) * CH)
            u = yi[sl, ds] + av[sl, ds] * dot(cm[sl, :], entry)
            yi[sl, ds] = u
            sq[sl, :] = sq[sl, :] + u * u
    fac[...] = jnp.broadcast_to(
        lax.rsqrt(jnp.sum(sq[...], axis=1, keepdims=True) * (1.0 / FEAT) + EPS), (TOK, 128)
    )

    writes = []
    for c in range(NCH):
        sl = slice(c * CH, (c + 1) * CH)

        def normed(nt, carry, sl=sl):
            ds = pl.ds(pl.multiple_of(nt * 128, 128), 128)
            out[sl, ds] = (yi[sl, ds] * fac[sl, :] * gains[:, ds]).astype(BF16)
            return carry

        lax.fori_loop(0, FEAT // 128, normed, 0)
        cp = pltpu.make_async_copy(out.at[sl], out_hbm.at[sl], out_sem.at[c])
        cp.start()
        writes.append(cp)

    mine = acc[pl.ds(pl.multiple_of(tp * 64, 64), 64), :]

    def p_sum(d, got):
        src = lax.rem(tp + TP - d, TP)
        p_copy(d, src, src).wait_recv()
        return got + p_recv[src].astype(F32)

    mine = lax.fori_loop(1, TP, p_sum, mine)
    for r in range(16):
        dec[r] = mine[r * STEPS:(r + 1) * STEPS, :].astype(BF16)

    for cp in writes:
        cp.wait()
    for cp in kv_send + q_send + o_sent:
        cp.wait_send()
    h_drain()
    f_drain()

    for peer in peers:
        for cp in (s_copy(peer), c_copy(peer, me), sc_copy(peer), e_copy(peer)):
            cp.wait_send()

    def drain_tp(d, c):
        p_copy(d, lax.rem(tp + d, TP), tp).wait_send()
        return c

    lax.fori_loop(1, TP, drain_tp, 0)


def on_device(
    prompt_mixer, prompt_gates, prompt_write, prompt_read, prompt_steps, decay_logs, skip_weights, norm_gains,
    prompt_keys, prompt_values, page_counts, decode_mixer, decode_gates, decode_write, decode_read, decode_steps,
    decode_queries, decode_keys, decode_values, mixer_output, attend_output,
):
    vmem = pl.BlockSpec(memory_space=pltpu.VMEM)
    smem = pl.BlockSpec(memory_space=pltpu.SMEM)
    v = pltpu.VMEM
    dma = pltpu.SemaphoreType.DMA
    scratch = [
        v((TOK, FEAT), BF16), v((TOK, FEAT), BF16), v((FEAT, COLS), BF16), v((ALLF - FEAT, COLS), BF16),
        v((TOK, FEAT), BF16), dma((4,)), dma((4,)),
        v((4, TOK, ATT_DIM), BF16), v((4, TOK, ATT_DIM), BF16), v((4, NQ, ATT_DIM), BF16),
        v((PAGES, RS, STATE), BF16),
        v((PAGES, STATE + 16, 128), BF16), v((PAGES, STATE + 16, 128), BF16),
        v((PAGES + 1, STATE, 128), BF16), v((PAGES, STATE, 128), BF16),
        v((PAGES, RS, 128), BF16), v((PAGES, RS, 128), BF16),
        v((4, ATT_DIM, NQ), BF16), v((4, ATT_DIM, NQ), BF16), v((4, 8, NQ), F32), v((4, 8, NQ), F32),
        v((PAGES, RS, ALLF), BF16), v((TP, 64, COLS), BF16), v((TP, 64, COLS), BF16),
        v((2 * HL, FEAT), BF16), v((STATE, TOK), BF16), v((NCH, CH, CH), BF16),
        v((TOK, 2 * HL), BF16), v((TOK, 2 * HL), BF16), v((TOK, 2 * HL), BF16),
        v((24, HL), F32), v((24, FEAT), F32),
        v((TOK, FEAT), F32), v((TOK, FEAT), F32), v((TOK, 128), F32), v((TOK, 128), F32),
        v((4 * TOK, NQ), F32), v((PAGES * RS, COLS), F32), v((PAGES * RS, 128), jnp.int32),
        v((PAGES * RS, PAGES * STATE), BF16),
        v((RS, FEAT), F32), v((RS, FEAT), F32), v((RS, STATE), F32), v((RS, STATE), F32), v((RS, HL), F32),
        v((RS, QH * ATT_DIM), F32), v((RS, ATT_DIM), F32), v((RS, ATT_DIM), F32), v((RS, FEAT), F32),
        dma((6,)), dma((6,)), dma((4,)), dma((4,)), dma((PAGES,)), dma((PAGES,)),
        dma((PAGES,)), dma((PAGES,)), dma((PAGES,)), dma((PAGES,)), dma((PAGES,)), dma((PAGES,)),
        dma((4,)), dma((4,)), dma((4,)), dma((4,)),
        dma((2, 4)), dma((2, 4)), dma((2, 4, 4)), dma((2, 4, 4)),
        dma((2, 4)), dma((2, 4)), dma((2, 4, 4)), dma((2, 4, 4)),
        dma((TP,)), dma((TP,)),
    ]
    hbm = pl.BlockSpec(memory_space=pl.ANY)
    specs = [hbm] * 2 + [vmem] * 8 + [smem] + [vmem] * 8 + [hbm] * 2
    return pl.pallas_call(
        kernel,
        out_shape=(
            jax.ShapeDtypeStruct((TOK, FEAT), BF16),
            jax.ShapeDtypeStruct((16, STEPS, COLS), BF16),
        ),
        in_specs=specs,
        out_specs=(hbm, vmem),
        scratch_shapes=scratch,
        compiler_params=pltpu.CompilerParams(
            collective_id=0, has_side_effects=True, vmem_limit_bytes=60 * 2**20
        ),
        name="layers",
    )(
        prompt_mixer, prompt_gates, prompt_write, prompt_read, prompt_steps.T,
        decay_logs.reshape(1, HL), skip_weights.reshape(1, HL), norm_gains.reshape(1, FEAT),
        prompt_keys, prompt_values, page_counts,
        decode_mixer, decode_gates, decode_write, decode_read, decode_steps,
        decode_queries, decode_keys, decode_values, mixer_output, attend_output,
    )


def solution(mesh):
    rows, heads = ("ctx", "section"), "tp"
    split = P(rows, heads)
    split3d = P(rows, None, heads)
    return jax.shard_map(
        on_device,
        mesh=mesh,
        in_specs=(split,) * 5 + (P(heads),) * 3 + (split,) * 2 + (P(),) + (split3d,) * 8 + (P(heads, rows),) * 2,
        out_specs=(split, P(heads, None, rows)),
        check_vma=False,
    )
```

```python
import jax
import jax.numpy as jnp
from jax import lax
from jax.experimental import pallas as pl
from jax.experimental.pallas import tpu as pltpu
from jax.sharding import PartitionSpec as P

HEADS, HEAD_DIM, STATE, GROUPS = 256, 64, 256, 8
QHEADS, KV_HEADS, ATT_DIM, STEPS = 64, 8, 128, 4
EPS = 1e-05
OFFSETS = ((2, 2), (1, 0), (0, 1), (3, 0), (0, 3), (2, 1), (1, 2), (2, 3), (3, 2), (1, 1), (3, 3), (1, 3), (3, 1), (2, 0), (0, 2))
NEG = -1e30
F32, BF16 = jnp.float32, jnp.bfloat16
MESH = pl.DeviceIdType.MESH

PAGES = 16
TOK = 512
HL = 32
FEAT = HL * HEAD_DIM
ROWS = 8
RS = ROWS * STEPS
CH = 128
NCH = TOK // CH
QH = QHEADS // KV_HEADS
NQ = QH * RS
TILE = 256
NT = FEAT // TILE
COLS = 512
TP = 8
ALLF = FEAT + QH * ATT_DIM
SCALE = ATT_DIM ** -0.5


def dot(a, b):
    return jnp.dot(a, b, preferred_element_type=F32)


def dot_t(a, b):
    return lax.dot_general(a, b, (((1,), (1,)), ((), ())), preferred_element_type=F32)


def dot_tn(a, b):
    return lax.dot_general(a, b, (((0,), (0,)), ((), ())), preferred_element_type=F32)


def split2(v):
    hi = v.astype(BF16)
    return hi, (v - hi.astype(F32)).astype(BF16)


def stack2(v):
    hi = v.astype(BF16).astype(F32)
    return jnp.concatenate([hi, v - hi], axis=1).astype(BF16)


def split3(v):
    hi = v.astype(BF16)
    rest = v - hi.astype(F32)
    mid = rest.astype(BF16)
    return hi, mid, (rest - mid.astype(F32)).astype(BF16)


def spot(x, z):
    return lax.div(z, 2) * 8 + x * 2 + lax.rem(z, 2)


def remote(src, dst, send, recv, device):
    return pltpu.make_async_remote_copy(
        src_ref=src, dst_ref=dst, send_sem=send, recv_sem=recv, device_id=device, device_id_type=MESH
    )


def kernel(
    x_hbm, gate_hbm, bm_hbm, cm_hbm, dt_hbm, dlog_hbm, skip_hbm, gains_hbm, keys_hbm, values_hbm, counts,
    xd_hbm, gd_hbm, bd_hbm, cd_hbm, dtd_hbm, qd_hbm, kd_hbm, vd_hbm, w1_hbm, w2_hbm,
    out_hbm, dec,
    bm, cm, dt_t, dlog, skip, gains, keys, values, xd, gd, bd, cd, dtd, qd, kd, vd, small_sem,
    x, gate, w1, w2, out, in_sem, out_sem,
    kbuf, vbuf, qbuf, cbuf, s_send, s_recv, pst, e_recv, sc_send, sc_recv,
    o_send, o_recv, t_send, t_recv, feat, p_send, p_recv, r_send, r_recv,
    exp_m, bt, mixg, a_w, b_w, end_w, small, rows, yi, av, sq, fac,
    scores, acc, cntb, picked, flat_x, flat_g, flat_b, flat_c, flat_dt, flat_q, flat_k, flat_v, ud,
    kv_ss, kv_rs, q_ss, q_rs, c_ss, c_rs, s_ss, s_rs, e_ss, e_rs, sc_ss, sc_rs,
    o_ss, o_rs, t_ss, t_rs, f1_ss, f1_rs, f2_ss, f2_rs, h1_ss, h1_rs, h2_ss, h2_rs, p_ss, p_rs, r_ss, r_rs,
):
    ctx, section = lax.axis_index("ctx"), lax.axis_index("section")
    tp = lax.axis_index("tp")
    me = ctx * 2 + section
    xi = lax.rem(ctx, 4)
    zi = lax.div(ctx, 4) * 2 + section
    xs = [xi] + [lax.rem(xi + d, 4) for d in range(1, 4)]
    zs = [zi] + [lax.rem(zi + d, 4) for d in range(1, 4)]
    z_ctx = [lax.div(z, 2) * 4 for z in zs]
    z_section = [lax.rem(z, 2) for z in zs]
    known = {}

    def off(dx, dz):
        key = (dx % 4, dz % 4)
        if key not in known:
            c = z_ctx[key[1]] + xs[key[0]]
            known[key] = (c * 2 + z_section[key[1]], {"ctx": c, "section": z_section[key[1]]})
        return known[key]

    def xpeer(d):
        return xs[d % 4]

    def zpeer(d):
        return zs[d % 4]

    ready = [
        pltpu.make_async_copy(src, dst, small_sem.at[i])
        for i, (src, dst) in enumerate((
            (qd_hbm, qd), (cd_hbm, cd), (keys_hbm, keys), (values_hbm, values), (dt_hbm, dt_t), (dlog_hbm, dlog),
            (skip_hbm, skip), (gains_hbm, gains), (bm_hbm, bm), (cm_hbm, cm), (xd_hbm, xd), (gd_hbm, gd), (bd_hbm, bd),
            (dtd_hbm, dtd), (kd_hbm, kd), (vd_hbm, vd),
        ))
    ]
    for cp in ready:
        cp.start()

    barrier = pltpu.get_barrier_semaphore()

    class Peer:
        def __init__(self, n, dx, dz):
            self.n = n
            self.to, self.to_place = off(dx, dz)
            self.back, self.back_place = off(-dx, -dz)

    peers = [Peer(n, dx, dz) for n, (dx, dz) in enumerate(OFFSETS)]
    for peer in peers:
        pl.semaphore_signal(barrier, inc=1, device_id=peer.to_place, device_id_type=MESH)
    tpeers = [lax.rem(tp + d, TP) for d in range(1, TP)]
    for t in tpeers:
        pl.semaphore_signal(barrier, inc=1, device_id={"tp": t}, device_id_type=MESH)

    loads = [
        pltpu.make_async_copy(src, dst, in_sem.at[i])
        for i, (src, dst) in enumerate(((x_hbm, x), (gate_hbm, gate), (w2_hbm, w2), (w1_hbm, w1)))
    ]
    for cp in loads:
        cp.start()

    for cp in ready:
        cp.wait()

    for r in range(ROWS):
        sl = slice(r * STEPS, (r + 1) * STEPS)
        flat_q[sl, :] = qd[r].astype(F32)
        flat_c[sl, :] = cd[r].astype(F32)
    for h in range(QH):
        qbuf[xi, h * RS:(h + 1) * RS, :] = flat_q[:, h * ATT_DIM:(h + 1) * ATT_DIM].astype(BF16)
    cbuf[me] = flat_c[...].astype(BF16)

    row_i = lax.broadcasted_iota(jnp.int32, (CH, CH), 0)
    col_i = lax.broadcasted_iota(jnp.int32, (CH, CH), 1)
    lower = row_i >= col_i
    tri = lower.astype(F32).astype(BF16)
    lane = lax.broadcasted_iota(jnp.int32, (2 * HL, FEAT), 1)
    head = lax.broadcasted_iota(jnp.int32, (2 * HL, FEAT), 0)
    start = jnp.where(head < HL, head, head - HL) * HEAD_DIM
    inside = jnp.logical_and(lane >= start, lane < start + HEAD_DIM)
    exp_m[...] = jnp.where(inside, 1.0, 0.0).astype(BF16)
    rate = jnp.exp(dlog[...])
    base = jnp.zeros((1, HL), F32)
    logs, steps = [], []
    for c in range(NCH):
        sl = slice(c * CH, (c + 1) * CH)
        step = jnp.transpose(dt_t[:, sl])
        hi, mid, lo = split3(-step * rate)
        log = dot(tri, hi) + dot(tri, mid) + dot(tri, lo)
        middle = log[CH // 2 - 1:CH // 2, :]
        last = log[CH - 1:CH, :]
        logs.append(base + log)
        steps.append(step)
        a_w[sl, :] = stack2(jnp.exp(log - middle))
        b_w[sl, :] = stack2(jnp.exp(middle - log) * step)
        small[c:c + 1, :] = jnp.exp(last)
        small[4 + c:5 + c, :] = jnp.exp(last - middle)
        small[8 + c:9 + c, :] = jnp.exp(middle)
        small[12 + c:13 + c, :] = jnp.exp(base + middle)
        base = base + last
    for c in range(NCH):
        sl = slice(c * CH, (c + 1) * CH)
        end_w[sl, :] = stack2(jnp.exp(base - logs[c]) * steps[c])
        bt[:, sl] = jnp.transpose(bm[sl, :].astype(F32)).astype(BF16)
    small[16:17, :] = jnp.exp(base)
    small[17:18, :] = skip[...]
    small[18:24, :] = jnp.zeros((6, HL), F32)
    hi, mid, lo = split3(small[...])
    one = exp_m[0:HL, :]
    rows[...] = dot(hi, one) + dot(mid, one) + dot(lo, one)

    pl.semaphore_wait(barrier, PAGES - 1 + TP - 1)

    up, down = off(0, 1)[1], off(0, 3)[1]
    kv_send, q_send = [], []

    def kv(buf, n, block, to, i):
        return remote(block, buf.at[n], kv_ss.at[i], kv_rs.at[i], to)


    loads[0].wait()

    def states(nt, carry):
        ds = pl.ds(pl.multiple_of(nt * TILE, TILE), TILE)
        e = exp_m[:, ds]
        xs = (x[:, ds].astype(F32) * dot(end_w[...], e)).astype(BF16)
        state = dot(bt[...], xs)
        sent = state.astype(BF16)
        hi, mid, lo = split3(rows[16:17, ds])
        which = lax.broadcasted_iota(jnp.int32, (16, TILE), 0)
        tail = jnp.where(
            which == 0, hi.astype(F32), jnp.where(which == 1, mid.astype(F32), jnp.where(which == 2, lo.astype(F32), 0.0))
        ).astype(BF16)
        for half in range(2):
            hs = slice(half * 128, (half + 1) * 128)
            s_send[2 * nt + half, 0:STATE, :] = sent[:, hs]
            s_send[2 * nt + half, STATE:STATE + 16, :] = tail[:, hs]
        return carry

    lax.fori_loop(0, NT, states, 0)

    def exchange(src, dst, send, recv):
        def copy(peer):
            return remote(src.at[peer.to], dst.at[me], send.at[peer.n], recv.at[peer.n], peer.to_place)

        def landed(peer):
            remote(src.at[peer.back], dst.at[peer.back], send.at[peer.n], recv.at[peer.n], peer.back_place).wait_recv()

        return copy, landed

    s_copy, s_landed = exchange(s_send, s_recv, s_ss, s_rs)
    sc_copy, sc_landed = exchange(sc_send, sc_recv, sc_ss, sc_rs)
    e_copy, e_landed = exchange(pst, e_recv, e_ss, e_rs)

    def c_copy(peer, src):
        return remote(cbuf.at[src], cbuf.at[src], c_ss.at[peer.n], c_rs.at[peer.n], peer.to_place)

    for peer in peers:
        s_copy(peer).start()
    for peer in peers:
        c_copy(peer, me).start()
    s_recv[me] = s_send[me]
    for d in (1, 3, 2):
        cp = remote(qbuf.at[xi], qbuf.at[xi], q_ss.at[d], q_rs.at[d], off(d, 0)[1])
        cp.start()
        q_send.append(cp)

    loads[1].wait()
    for c in range(NCH):
        sl = slice(c * CH, (c + 1) * CH)
        mixg[c] = jnp.where(lower, dot_t(cm[sl, :], bm[sl, :]), 0.0).astype(BF16)

    def within(nt, carry):
        ds = pl.ds(pl.multiple_of(nt * TILE, TILE), TILE)
        e = exp_m[:, ds]
        state = None
        for c in range(NCH):
            sl = slice(c * CH, (c + 1) * CH)
            xf = x[sl, ds].astype(F32)
            xs = (xf * dot(b_w[sl, :], e)).astype(BF16)
            y = dot(mixg[c], xs)
            if c > 0:
                y = y + rows[8 + c:9 + c, ds] * dot(cm[sl, :], state.astype(BF16))
            if c < NCH - 1:
                fresh = rows[4 + c:5 + c, ds] * dot(bt[:, sl], xs)
                state = fresh if c == 0 else rows[c:c + 1, ds] * state + fresh
            a = dot(a_w[sl, :], e)
            g = gate[sl, ds].astype(F32)
            g = g / (1.0 + jnp.exp(-g))
            yi[sl, ds] = g * (a * y + rows[17:18, ds] * xf)
            av[sl, ds] = g * (a * rows[12 + c:13 + c, ds])
        return carry

    lax.fori_loop(0, NT, within, 0)

    for peer in peers:
        c_copy(peer, peer.back).wait_recv()

    def fill(i, c):
        which = lax.broadcasted_iota(jnp.int32, (8, 128), 0)
        cntb[pl.ds(pl.multiple_of(i * 8, 8), 8), :] = jnp.where(which < 4, counts[2 * i], counts[2 * i + 1])
        return c

    lax.fori_loop(0, PAGES * ROWS // 2, fill, 0)

    def mask_reads(k, c):
        for q in range(4):
            sl = slice(q * 128, (q + 1) * 128)
            reads = cbuf[q * 4:(q + 1) * 4].reshape(128, STATE).astype(F32)
            want = cntb[sl, :] == k + 1
            for half in range(2):
                hs = slice(half * 128, (half + 1) * 128)
                at = pl.ds(pl.multiple_of(k * STATE + half * 128, 128), 128)
                picked[sl, at] = jnp.where(want, reads[:, hs], 0.0).astype(BF16)
        return c

    lax.fori_loop(0, PAGES, mask_reads, 0)

    for r in range(ROWS):
        sl = slice(r * STEPS, (r + 1) * STEPS)
        flat_k[sl, :] = kd[r].astype(F32)
        flat_v[sl, :] = vd[r].astype(F32)
        flat_x[sl, :] = xd[r].astype(F32)
        flat_g[sl, :] = gd[r].astype(F32)
        flat_b[sl, :] = bd[r].astype(F32)
        flat_dt[sl, :] = dtd[r]
    tok_r = lax.broadcasted_iota(jnp.int32, (RS, RS), 0)
    tok_c = lax.broadcasted_iota(jnp.int32, (RS, RS), 1)
    same = jnp.logical_and(tok_r // STEPS == tok_c // STEPS, tok_r >= tok_c)
    same_b = same.astype(F32).astype(BF16)
    hi, mid, lo = split3(-flat_dt[...] * rate)
    log = dot(same_b, hi) + dot(same_b, mid) + dot(same_b, lo)
    ad_w = stack2(jnp.exp(log))
    bd_w = stack2(jnp.exp(-log) * flat_dt[...])
    own = jnp.where(same, dot_t(flat_c[...].astype(BF16), flat_b[...].astype(BF16)), 0.0).astype(BF16)

    for nt in range(NT):
        ds = slice(nt * TILE, (nt + 1) * TILE)
        e = exp_m[:, ds]
        xt = flat_x[:, ds]
        ws = (xt * dot(bd_w, e)).astype(BF16)
        g = flat_g[:, ds]
        g = g / (1.0 + jnp.exp(-g))
        a = dot(ad_w, e)
        ud[:, ds] = g * (a * dot(own, ws) + rows[17:18, ds] * xt)
        flat_g[:, ds] = g * a

    def gather(start, width, s1, r1, s2, r2):
        half = width // 2
        cols = (pl.ds(start, half), pl.ds(start + half, half))

        def peer(a, d):
            return off(0, d) if a == 0 else off(d, 0)

        def block(p, a):
            return feat.at[p, :, cols[a]]

        sent = []

        def go(p, a, send, recv, to):
            cp = remote(block(p, a), block(p, a), send, recv, to[1])
            cp.start()
            sent.append(cp)

        def forward(p, a, k):
            for d in (1, 3, 2):
                go(p, a, s2.at[a, k, d], r2.at[a, k, d], peer(1 - a, d))

        def first():
            for d in (1, 3, 2):
                for a in (0, 1):
                    go(me, a, s1.at[a, d], r1.at[a, d], peer(a, d))
            for a in (0, 1):
                forward(me, a, 0)

        def second():
            for d in (1, 3, 2):
                for a in (0, 1):
                    p, where = peer(a, -d)
                    remote(block(p, a), block(p, a), s1.at[a, d], r1.at[a, d], where).wait_recv()
                    forward(p, a, d)

        def finish():
            for k in (0, 1, 3, 2):
                for d in (1, 3, 2):
                    for a in (0, 1):
                        p = (off(-d, -k) if a == 0 else off(-k, -d))[0]
                        where = peer(1 - a, -d)[1]
                        remote(block(p, a), block(p, a), s2.at[a, k, d], r2.at[a, k, d], where).wait_recv()

        def drain():
            for cp in sent:
                cp.wait_send()

        return first, second, finish, drain

    h_first, h_second, h_finish, h_drain = gather(FEAT, ALLF - FEAT, h1_ss, h1_rs, h2_ss, h2_rs)
    f_first, f_second, f_finish, f_drain = gather(0, FEAT, f1_ss, f1_rs, f2_ss, f2_rs)
    for peer in peers:
        s_landed(peer)
    for i, (src, buf) in enumerate(((keys, kbuf), (values, vbuf))):
        for k, to in ((0, up), (1, down)):
            cp = kv(buf, zi, src, to, 2 * i + k)
            cp.start()
            kv_send.append(cp)
    kbuf[zi] = keys[...]
    vbuf[zi] = values[...]
    pst[0] = jnp.zeros((STATE, 128), BF16)

    def scan(k, state):
        tail = s_recv[k, STATE:STATE + 16, :].astype(F32)
        decay = tail[0:1, :] + tail[1:2, :] + tail[2:3, :]
        state = decay * state + s_recv[k, 0:STATE, :].astype(F32)
        pst[k + 1] = state.astype(BF16)
        return state

    lax.fori_loop(0, PAGES, scan, jnp.zeros((STATE, 128), F32), unroll=4)

    for q in range(2):
        sl = slice(q * 256, (q + 1) * 256)
        got = dot(picked[sl, :], pst[1:PAGES + 1].reshape(PAGES * STATE, 128))
        sc_send[q * 8:(q + 1) * 8] = got.astype(BF16).reshape(8, RS, 128)

    for peer in peers:
        sc_copy(peer).start()
    sc_recv[me] = sc_send[me]

    kv(kbuf, zpeer(3), keys, up, 0).wait_recv()
    cp = kv(kbuf, zpeer(3), kbuf.at[zpeer(3)], up, 4)
    cp.start()
    kv_send.append(cp)
    kv(vbuf, zpeer(1), values, down, 3).wait_recv()
    cp = kv(vbuf, zpeer(1), vbuf.at[zpeer(1)], down, 5)
    cp.start()
    kv_send.append(cp)

    e_recv[me] = pst[me]

    for peer in peers:
        sc_landed(peer)
    square = jnp.zeros((RS, TILE), F32)
    for nt in range(NT):
        ds = slice(nt * TILE, (nt + 1) * TILE)
        past = jnp.concatenate([sc_recv[2 * nt], sc_recv[2 * nt + 1]], axis=1).astype(F32)
        u = ud[:, ds] + flat_g[:, ds] * past
        ud[:, ds] = u
        square = square + u * u
    scale = lax.rsqrt(jnp.sum(square, axis=1, keepdims=True) * (1.0 / FEAT) + EPS)
    feat[me, :, 0:FEAT] = (ud[...] * scale * gains[...]).astype(BF16)
    f_first()

    kv(kbuf, zpeer(1), keys, down, 1).wait_recv()
    kv(vbuf, zpeer(3), values, up, 2).wait_recv()
    kv(kbuf, zpeer(2), keys, up, 4).wait_recv()
    kv(vbuf, zpeer(2), values, down, 5).wait_recv()
    for d in (1, 3, 2):
        xsrc = xpeer(4 - d)
        remote(qbuf.at[xsrc], qbuf.at[xsrc], q_ss.at[d], q_rs.at[d], off(-d, 0)[1]).wait_recv()

    token_of = lax.rem(lax.broadcasted_iota(jnp.int32, (1, NQ), 1), RS)
    row_of = token_of // STEPS

    def attend(i, carry):
        queries = qbuf[i]
        first = spot(i, zi) * ROWS
        seen = jnp.zeros((1, NQ), jnp.int32)
        for r in range(ROWS):
            seen = jnp.where(row_of == r, counts[first + r], seen)
        tops = []
        for z in range(4):
            bias = jnp.where(spot(xi, z) < seen, 0.0, NEG)
            for b in range(TOK // CH):
                s = dot_t(kbuf[z, b * CH:(b + 1) * CH, :], queries) + bias
                at = z * TOK + b * CH
                scores[at:at + CH, :] = s
                tops.append(jnp.max(s.reshape(CH // 8, 8, NQ), axis=0))
        while len(tops) > 1:
            tops = [jnp.maximum(p, q) for p, q in zip(tops[::2], tops[1::2])]
        top = jnp.max(tops[0], axis=0, keepdims=True)
        total = jnp.zeros((8, NQ), F32)
        summed = jnp.zeros((ATT_DIM, NQ), F32)
        for z in range(4):
            for b in range(TOK // CH):
                at = z * TOK + b * CH
                w = jnp.exp((scores[at:at + CH, :] - top) * SCALE)
                total = total + jnp.sum(w.reshape(CH // 8, 8, NQ), axis=0)
                summed = summed + dot_tn(vbuf[z, b * CH:(b + 1) * CH, :], w.astype(BF16))
        o_send[i] = summed.astype(BF16)
        which = lax.broadcasted_iota(jnp.int32, (8, NQ), 0)
        t_send[i] = jnp.where(which == 0, top, jnp.sum(total, axis=0, keepdims=True))
        return carry

    lax.fori_loop(0, 2, attend, 0)
    f_second()
    for peer in peers:
        e_copy(peer).start()
    lax.fori_loop(2, 4, attend, 0)

    o_sent = []
    for d in (1, 3, 2):
        xp_d = xpeer(d)
        dx = off(d, 0)[1]
        for src, dst, ss, rs in ((o_send, o_recv, o_ss, o_rs), (t_send, t_recv, t_ss, t_rs)):
            cp = remote(src.at[xp_d], dst.at[xi], ss.at[d], rs.at[d], dx)
            cp.start()
            o_sent.append(cp)
    o_recv[xi] = o_send[xi]
    t_recv[xi] = t_send[xi]

    f_finish()
    loads[3].wait()

    def project(q, c):
        lhs = feat[pl.ds(q * 4, 4), :, 0:FEAT].reshape(128, FEAT)
        acc[pl.ds(pl.multiple_of(q * 128, 128), 128), :] = dot(lhs, w1[...])
        return c

    lax.fori_loop(0, 4, project, 0)

    key_i = lax.broadcasted_iota(jnp.int32, (RS, NQ), 0)
    tok_i = lax.rem(lax.broadcasted_iota(jnp.int32, (RS, NQ), 1), RS)
    near_ok = jnp.logical_and(key_i // STEPS == tok_i // STEPS, key_i <= tok_i)
    near = jnp.where(near_ok, dot_t(flat_k[...].astype(BF16), qbuf[xi]), NEG)
    for d in (1, 3, 2):
        xsrc = xpeer(4 - d)
        dx = off(-d, 0)[1]
        remote(o_send.at[xsrc], o_recv.at[xsrc], o_ss.at[d], o_rs.at[d], dx).wait_recv()
        remote(t_send.at[xsrc], t_recv.at[xsrc], t_ss.at[d], t_rs.at[d], dx).wait_recv()
    top = jnp.max(near, axis=0, keepdims=True)
    for i in range(4):
        top = jnp.maximum(top, t_recv[i, 0:1, :])
    w = jnp.where(near_ok, jnp.exp((near - top) * SCALE), 0.0)
    total = jnp.sum(w, axis=0, keepdims=True)
    summed = dot_tn(flat_v[...].astype(BF16), w.astype(BF16))
    for i in range(4):
        part = jnp.exp((t_recv[i, 0:1, :] - top) * SCALE)
        total = total + part * t_recv[i, 1:2, :]
        summed = summed + part * o_recv[i].astype(F32)
    att = jnp.transpose(summed / total)
    for h in range(QH):
        feat[me, :, FEAT + h * ATT_DIM:FEAT + (h + 1) * ATT_DIM] = att[h * RS:(h + 1) * RS, :].astype(BF16)

    h_first()

    sq[...] = jnp.zeros((TOK, 128), F32)

    def across(n):
        if n > 0:
            e_landed(peers[n - 1])
        src = me if n == 0 else peers[n - 1].back
        ds = pl.ds(pl.multiple_of(src * 128, 128), 128)
        entry = e_recv[src]
        for c in range(NCH):
            sl = slice(c * CH, (c + 1) * CH)
            u = yi[sl, ds] + av[sl, ds] * dot(cm[sl, :], entry)
            yi[sl, ds] = u
            sq[sl, :] = sq[sl, :] + u * u

    for n in range(8):
        across(n)
    h_second()
    for n in range(8, PAGES):
        across(n)

    h_finish()
    loads[2].wait()

    core, yi_here = lax.rem(tp, 2), lax.div(tp, 2)
    order = (1, 3, 2, 0)

    def p1_copy(turn, q):
        return remote(
            p_send.at[2 * q + 1 - core], p_recv.at[turn], p_ss.at[turn], p_rs.at[turn], {"tp": 2 * yi_here + 1 - core}
        )

    def p2_copy(turn, q):
        return remote(r_send.at[turn], r_recv.at[turn], r_ss.at[turn], r_rs.at[turn], {"tp": 2 * q + core})

    def both_cores(turn, q):
        p1_copy(turn, q).wait_recv()
        return acc[pl.ds(pl.multiple_of((2 * q + core) * 64, 64), 64), :] + p_recv[turn].astype(F32)

    owners = [lax.rem(yi_here + turn, 4) for turn in range(4)]
    for turn in order:
        q = owners[turn]
        at = pl.ds(pl.multiple_of(q * 128, 128), 128)
        lhs = feat[pl.ds(q * 4, 4), :, FEAT:ALLF].reshape(128, ALLF - FEAT)
        part = acc[at, :] + dot(lhs, w2[...])
        acc[at, :] = part
        p_send[pl.ds(2 * q, 2)] = part.astype(BF16).reshape(2, 64, COLS)
        p1_copy(turn, q).start()
    for turn in order[:3]:
        r_send[turn] = both_cores(turn, owners[turn]).astype(BF16)
        p2_copy(turn, owners[turn]).start()

    fac[...] = jnp.broadcast_to(
        lax.rsqrt(jnp.sum(sq[...], axis=1, keepdims=True) * (1.0 / FEAT) + EPS), (TOK, 128)
    )

    writes = []
    for c in range(NCH):
        sl = slice(c * CH, (c + 1) * CH)

        def normed(nt, carry, sl=sl):
            ds = pl.ds(pl.multiple_of(nt * 128, 128), 128)
            out[sl, ds] = (yi[sl, ds] * fac[sl, :] * gains[:, ds]).astype(BF16)
            return carry

        lax.fori_loop(0, FEAT // 128, normed, 0)
        cp = pltpu.make_async_copy(out.at[sl], out_hbm.at[sl], out_sem.at[c])
        cp.start()
        writes.append(cp)

    mine = both_cores(0, owners[0])
    for turn in order[:3]:
        p2_copy(turn, owners[turn]).wait_recv()
        mine = mine + r_recv[turn].astype(F32)
    for r in range(16):
        dec[r] = mine[r * STEPS:(r + 1) * STEPS, :].astype(BF16)

    for cp in writes:
        cp.wait()
    for cp in kv_send + q_send + o_sent:
        cp.wait_send()
    h_drain()
    f_drain()

    for peer in peers:
        for cp in (s_copy(peer), c_copy(peer, me), sc_copy(peer), e_copy(peer)):
            cp.wait_send()

    for turn in order:
        p1_copy(turn, owners[turn]).wait_send()
        if turn > 0:
            p2_copy(turn, owners[turn]).wait_send()


def hand_over(a, b, a_out, b_out, a_held, b_held, in_sem, out_sem):
    rows = TOK // 8
    slices = [pl.ds(i * rows, rows) for i in range(8)]
    pairs = [(a.at[sl], a_held.at[sl], a_out.at[sl]) for sl in slices] + [(b, b_held, b_out)]
    inward = [pltpu.make_async_copy(src, held, in_sem.at[i]) for i, (src, held, _) in enumerate(pairs)]
    outward = [pltpu.make_async_copy(held, dst, out_sem.at[i]) for i, (_, held, dst) in enumerate(pairs)]
    for cp in inward:
        cp.start()
    for arrived, leaving in zip(inward, outward):
        arrived.wait()
        leaving.start()
    for cp in outward:
        cp.wait()


def on_device(
    prompt_mixer, prompt_gates, prompt_write, prompt_read, prompt_steps, decay_logs, skip_weights, norm_gains,
    prompt_keys, prompt_values, page_counts, decode_mixer, decode_gates, decode_write, decode_read, decode_steps,
    decode_queries, decode_keys, decode_values, mixer_output, attend_output,
):
    vmem = pl.BlockSpec(memory_space=pltpu.VMEM)
    smem = pl.BlockSpec(memory_space=pltpu.SMEM)
    v = pltpu.VMEM
    dma = pltpu.SemaphoreType.DMA
    scratch = [
        v((TOK, STATE), BF16), v((TOK, STATE), BF16), v((HL, TOK), F32), v((1, HL), F32), v((1, HL), F32), v((1, FEAT), F32),
        v((TOK, ATT_DIM), BF16), v((TOK, ATT_DIM), BF16),
        v((ROWS, STEPS, FEAT), BF16), v((ROWS, STEPS, FEAT), BF16),
        v((ROWS, STEPS, STATE), BF16), v((ROWS, STEPS, STATE), BF16), v((ROWS, STEPS, HL), F32),
        v((ROWS, STEPS, QH * ATT_DIM), BF16), v((ROWS, STEPS, ATT_DIM), BF16), v((ROWS, STEPS, ATT_DIM), BF16), dma((16,)),
        v((TOK, FEAT), BF16), v((TOK, FEAT), BF16), v((FEAT, COLS), BF16), v((ALLF - FEAT, COLS), BF16),
        v((TOK, FEAT), BF16), dma((4,)), dma((4,)),
        v((4, TOK, ATT_DIM), BF16), v((4, TOK, ATT_DIM), BF16), v((4, NQ, ATT_DIM), BF16),
        v((PAGES, RS, STATE), BF16),
        v((PAGES, STATE + 16, 128), BF16), v((PAGES, STATE + 16, 128), BF16),
        v((PAGES + 1, STATE, 128), BF16), v((PAGES, STATE, 128), BF16),
        v((PAGES, RS, 128), BF16), v((PAGES, RS, 128), BF16),
        v((4, ATT_DIM, NQ), BF16), v((4, ATT_DIM, NQ), BF16), v((4, 8, NQ), F32), v((4, 8, NQ), F32),
        v((PAGES, RS, ALLF), BF16), v((TP, 64, COLS), BF16),
        v((4, 64, COLS), BF16), v((4, 64, COLS), BF16), v((4, 64, COLS), BF16),
        v((2 * HL, FEAT), BF16), v((STATE, TOK), BF16), v((NCH, CH, CH), BF16),
        v((TOK, 2 * HL), BF16), v((TOK, 2 * HL), BF16), v((TOK, 2 * HL), BF16),
        v((24, HL), F32), v((24, FEAT), F32),
        v((TOK, FEAT), F32), v((TOK, FEAT), F32), v((TOK, 128), F32), v((TOK, 128), F32),
        v((4 * TOK, NQ), F32), v((PAGES * RS, COLS), F32), v((PAGES * RS, 128), jnp.int32),
        v((PAGES * RS, PAGES * STATE), BF16),
        v((RS, FEAT), F32), v((RS, FEAT), F32), v((RS, STATE), F32), v((RS, STATE), F32), v((RS, HL), F32),
        v((RS, QH * ATT_DIM), F32), v((RS, ATT_DIM), F32), v((RS, ATT_DIM), F32), v((RS, FEAT), F32),
        dma((6,)), dma((6,)), dma((4,)), dma((4,)), dma((PAGES,)), dma((PAGES,)),
        dma((PAGES,)), dma((PAGES,)), dma((PAGES,)), dma((PAGES,)), dma((PAGES,)), dma((PAGES,)),
        dma((4,)), dma((4,)), dma((4,)), dma((4,)),
        dma((2, 4)), dma((2, 4)), dma((2, 4, 4)), dma((2, 4, 4)),
        dma((2, 4)), dma((2, 4)), dma((2, 4, 4)), dma((2, 4, 4)),
        dma((4,)), dma((4,)), dma((4,)), dma((4,)),
    ]
    hbm = pl.BlockSpec(memory_space=pl.ANY)
    specs = [hbm] * 10 + [smem] + [hbm] * 10
    shapes = (jax.ShapeDtypeStruct((TOK, FEAT), BF16), jax.ShapeDtypeStruct((16, STEPS, COLS), BF16))
    results = pl.pallas_call(
        kernel,
        out_shape=shapes,
        in_specs=specs,
        out_specs=(hbm, vmem),
        scratch_shapes=scratch,
        compiler_params=pltpu.CompilerParams(
            collective_id=0, has_side_effects=True, vmem_limit_bytes=60 * 2**20
        ),
        name="layers",
    )(
        prompt_mixer, prompt_gates, prompt_write, prompt_read, prompt_steps.T,
        decay_logs.reshape(1, HL), skip_weights.reshape(1, HL), norm_gains.reshape(1, FEAT),
        prompt_keys, prompt_values, page_counts,
        decode_mixer, decode_gates, decode_write, decode_read, decode_steps,
        decode_queries, decode_keys, decode_values, mixer_output, attend_output,
    )
    return pl.pallas_call(
        hand_over,
        out_shape=shapes,
        in_specs=[hbm, hbm],
        out_specs=(hbm, hbm),
        scratch_shapes=[v((TOK, FEAT), BF16), v((16, STEPS, COLS), BF16), dma((9,)), dma((9,))],
        name="results",
    )(*results)


def solution(mesh):
    rows, heads = ("ctx", "section"), "tp"
    split = P(rows, heads)
    split3d = P(rows, None, heads)
    return jax.shard_map(
        on_device,
        mesh=mesh,
        in_specs=(split,) * 5 + (P(heads),) * 3 + (split,) * 2 + (P(),) + (split3d,) * 8 + (P(heads, rows),) * 2,
        out_specs=(split, P(heads, None, rows)),
        check_vma=False,
    )
```
